256 devices in a mesh: node: 4 (over x), local: 64 (over z, y, core).
Axes of the slice: x: 4, y: 4, z: 8, core: 2. Of those that a mesh axis runs over, the one named last changes fastest.
Arguments:
- query: bfloat16 [32768, 1024], P(('node', 'local')), may hold values from -40 to 40
- key: bfloat16 [32768, 128], P(('node', 'local')), may hold values from -4 to 4
- value: bfloat16 [32768, 128], P(('node', 'local')), may hold values from -6 to 6
- grad_out: bfloat16 [32768, 1024], P(('node', 'local')), may hold values from -6 to 6
- stretch_order: int32 [4, 128], replicated, may hold values from 0 to 127, each once within a row
- reach: int32 [4], replicated, may hold values from 1024 to 2048, as said below
Outputs:
- grad_query: bfloat16 [32768, 1024], P(('node', 'local'))
- grad_key: bfloat16 [32768, 128], P(('node', 'local'))
- grad_value: bfloat16 [32768, 128], P(('node', 'local'))
The draws below stay inside these ranges and needn't reach their ends.
Inputs may be any that keep to these rules, and one draw needn't show every extreme that they name: `stretch_order`: each row is a permutation of 0 to 127. Some block has reach exactly 2048.
All inputs are finite; a program needn't handle non-finite values.
Results may differ from the reference program's by a relative error of at most 0.04.
Values may be sent and summed in bfloat16 or wider, within the bound.
No kernel may reach another device: no remote copies, remote signals or barrier semaphores. Data moves between devices by JAX's collectives and lax.ppermute only.
A program may use at most 128 MiB of HBM per device.

```python
import jax
import jax.numpy as jnp
from jax import lax

HEADS = 8
HEAD_DIM = 128
STRETCH_LEN = 64
BLOCK = 8192
STRETCHES = 128
REACH_STRETCHES = 32
WINDOW = 2112
TOKENS = 32768
N_NODE = 4


def key_base(key):
    sample = jax.random.normal(key, (TOKENS, HEAD_DIM), jnp.float32)
    return jnp.clip(sample, -4.0, 4.0)


def draw_key(key, part):
    base = key_base(key)
    return base.astype(jnp.bfloat16)


def draw_query(key, part):
    key = jax.random.fold_in(key, 12)
    noise = jnp.clip(jax.random.normal(key, (TOKENS, HEADS, HEAD_DIM), jnp.float32), -4.0, 4.0)
    return noise.reshape(TOKENS, HEADS * HEAD_DIM).astype(jnp.bfloat16)


def draw_reach(key, part):
    key = jax.random.fold_in(key, 13)
    first, second = jax.random.split(key)
    values = jax.random.randint(first, (N_NODE,), BLOCK // 8, BLOCK // 4 + 1, jnp.int32)
    where_full = jax.random.randint(second, (), 0, N_NODE, jnp.int32)
    return jnp.where(jnp.arange(N_NODE, dtype=jnp.int32) == where_full, BLOCK // 4, values).astype(jnp.int32)


def level_of(own_key, shape, pieces, low, top_value):
    loudness, own = 1.0, jax.random.fold_in(own_key, 6)
    for dim, shards_of in pieces:
        draws = jnp.exp(jax.random.uniform(jax.random.fold_in(own, dim), (shards_of,), jnp.float32, low / len(pieces), top_value / len(pieces)))
        loudness = loudness * jnp.repeat(draws, shape[dim] // shards_of).reshape([-1 if axis == dim else 1 for axis in range(len(shape))])
    return loudness


def bell_draw(key, dims, scale, bound, cuts=(), kind=jnp.bfloat16):
    result = jax.random.normal(key, dims, jnp.float32) * scale
    if len(cuts) > 0:
        result = level_of(key, dims, cuts, -0.22, 0.18) * result
    return jnp.clip(result, min=-bound, max=bound).astype(kind)


def setup_inputs(seed: int = 0) -> dict:
    key_list = jax.random.split(jax.random.key(seed), 7)
    return {
        "query": draw_query(jax.random.fold_in(key_list[6], 71), 0),
        "key": draw_key(jax.random.fold_in(key_list[6], 71), 0),
        "value": bell_draw(key_list[2], (TOKENS, HEAD_DIM), 1.0, 6.0, ((0, 256),)),
        "grad_out": bell_draw(key_list[3], (TOKENS, HEADS * HEAD_DIM), 1.0, 6.0, ((0, 256),)),
        "stretch_order": jax.vmap(lambda own: jax.random.permutation(own, STRETCHES))(jax.random.split(key_list[4], N_NODE)).reshape((N_NODE, STRETCHES)).astype(jnp.int32),
        "reach": draw_reach(jax.random.fold_in(key_list[6], 71), 0),
    }


def token_positions(stretch_order):
    slots = jnp.arange(BLOCK, dtype=jnp.int32)
    table = stretch_order[:, slots // STRETCH_LEN].astype(jnp.int32)
    base = (jnp.arange(N_NODE, dtype=jnp.int32) * BLOCK)[:, None]
    return base + table * STRETCH_LEN + slots[None, :] % STRETCH_LEN


def block_grads(queries, douts, keys, values, q_pos, k_pos, reach_now):
    scale = 1.0 / (HEAD_DIM ** 0.5)
    q32 = queries.astype(jnp.float32)
    d32 = douts.astype(jnp.float32)
    k32 = keys.astype(jnp.float32)
    v32 = values.astype(jnp.float32)
    scores = jnp.einsum("thd,kd->htk", q32, k32) * scale
    seen = (k_pos[None, :] <= q_pos[:, None]) & (k_pos[None, :] >= q_pos[:, None] - reach_now) & (k_pos[None, :] >= 0)
    seen = seen[None]
    peak = jnp.max(jnp.where(seen, scores, -1e30), axis=-1)
    expd = jnp.where(seen, jnp.exp(scores - peak[..., None]), 0.0)
    total = jnp.sum(expd, axis=-1)
    prob = expd / total[..., None]
    prob_b = prob.astype(jnp.bfloat16)
    attended = jnp.einsum("htk,kd->thd", prob_b.astype(jnp.float32), v32).astype(jnp.bfloat16)
    delta = jnp.sum(d32 * attended.astype(jnp.float32), axis=-1).T
    dprob = jnp.einsum("thd,kd->htk", d32, v32)
    dscore = (prob * (dprob - delta[..., None])).astype(jnp.bfloat16).astype(jnp.float32)
    grad_v = jnp.einsum("htk,thd->kd", prob_b.astype(jnp.float32), d32)
    grad_k = jnp.einsum("htk,thd->kd", dscore, q32) * scale
    grad_q = jnp.einsum("htk,kd->thd", dscore, k32) * scale
    return grad_q, grad_k, grad_v


def reference(query, key, value, grad_out, stretch_order, reach):
    stretch_total = TOKENS // STRETCH_LEN
    positions = token_positions(stretch_order).reshape(stretch_total, STRETCH_LEN)
    inverse = jnp.argsort(stretch_order, axis=1).astype(jnp.int32)
    key_c = key.reshape(stretch_total, STRETCH_LEN, HEAD_DIM)
    value_c = value.reshape(stretch_total, STRETCH_LEN, HEAD_DIM)
    query4 = query.reshape(stretch_total, STRETCH_LEN, HEADS, HEAD_DIM)
    dout4 = grad_out.reshape(stretch_total, STRETCH_LEN, HEADS, HEAD_DIM)
    steps = jnp.arange(REACH_STRETCHES + 1, dtype=jnp.int32)
    inner = jnp.arange(STRETCH_LEN, dtype=jnp.int32)

    def one_stretch(carry, stretch_idx):
        gk_acc, gv_acc = carry
        blk = (stretch_idx // STRETCHES).astype(jnp.int32)
        slot = (stretch_idx % STRETCHES).astype(jnp.int32)
        seq = blk * STRETCHES + stretch_order[blk, slot].astype(jnp.int32)
        wanted = seq - REACH_STRETCHES + steps
        valid = wanted >= 0
        safe = jnp.maximum(wanted, 0).astype(jnp.int32)
        src = ((safe // STRETCHES) * STRETCHES + inverse[safe // STRETCHES, safe % STRETCHES]).astype(jnp.int32)
        keys = key_c[src].reshape(WINDOW, HEAD_DIM)
        values = value_c[src].reshape(WINDOW, HEAD_DIM)
        k_pos = jnp.where(valid[:, None], safe[:, None] * STRETCH_LEN + inner[None, :], -1).reshape(WINDOW).astype(jnp.int32)
        grad_q, grad_k, grad_v = block_grads(query4[stretch_idx], dout4[stretch_idx], keys, values, positions[stretch_idx], k_pos, reach[blk])
        gk_acc = gk_acc.at[src].add(grad_k.reshape(REACH_STRETCHES + 1, STRETCH_LEN, HEAD_DIM))
        gv_acc = gv_acc.at[src].add(grad_v.reshape(REACH_STRETCHES + 1, STRETCH_LEN, HEAD_DIM))
        return (gk_acc, gv_acc), grad_q

    empty = jnp.zeros((stretch_total, STRETCH_LEN, HEAD_DIM), jnp.float32)
    (grad_k, grad_v), grad_q = lax.scan(one_stretch, (empty, empty), jnp.arange(stretch_total, dtype=jnp.int32))
    grad_query = grad_q.reshape(TOKENS, HEADS * HEAD_DIM).astype(jnp.bfloat16)
    grad_key = grad_k.reshape(TOKENS, HEAD_DIM).astype(jnp.bfloat16)
    grad_value = grad_v.reshape(TOKENS, HEAD_DIM).astype(jnp.bfloat16)
    return (grad_query, grad_key, grad_value)
```

```python
import functools

import jax
import jax.numpy as jnp
import numpy as np
from jax import lax
from jax.experimental import pallas as pl
from jax.experimental.pallas import tpu as pltpu
from jax.sharding import PartitionSpec as P

HEAD_DIM = 128
PAIR = 2 * HEAD_DIM
HEADS = 8
STRETCH = 64
SLOTS = 128
BACK = 32
KEYS = BACK + 1
WINDOW = KEYS * STRETCH
COLS = HEADS * STRETCH
CHUNK = 11 * STRETCH
CHUNKS = WINDOW // CHUNK
TAIL = BACK // 2
NZ, NY = 8, 4
LOCAL = NZ * NY * 2
FAR = -1e30

MEMBERS = (((2, 1), (6, 1)), ((6, 3), (2, 3)), ((0, 2), (4, 0)))
OPPOSITE = (4, 2)


def local_of(z, y, c):
    return ((z % NZ) * NY + y % NY) * 2 + c


def moves(by_core):
    out = []
    for source in range(LOCAL):
        z, y, c = source // (NY * 2), (source // 2) % NY, source % 2
        if by_core is None:
            out.append((source, local_of(z, y, 1 - c)))
        else:
            dz, dy = by_core[c]
            out.append((source, local_of(z + dz, y + dy, c)))
    return out


def send(value, by_core):
    return lax.ppermute(value, "local", moves(by_core))


def swap(value):
    return send(value, None)


def shift(value, dz, dy):
    return send(value, ((dz, dy), (dz, dy)))


def gather_block(own, unit, send, join):
    swap = functools.partial(send, by_core=None)
    chip = join([own, swap(own)])
    members = [send(chip, by_core=m) for m in MEMBERS]
    opposite = send(own, by_core=(OPPOSITE, OPPOSITE))
    mine = join([own, opposite] + members)
    half = 4 * unit
    up = send(mine[:half], by_core=((0, 1), (0, 1)))
    down = send(mine[:half], by_core=((0, -1), (0, -1)))
    ahead = send(mine, by_core=((1, 0), (1, 0)))
    behind = send(mine, by_core=((-1, 0), (-1, 0)))
    pieces = [mine, up, down, ahead, behind]
    return pieces + [swap(piece) for piece in pieces]


def piece_table():
    labels = np.arange(SLOTS).reshape(LOCAL, 2).T

    def fake_send(value, by_core):
        out = np.empty_like(value)
        for source, target in moves(by_core):
            out[:, target] = value[:, source]
        return out

    pieces = gather_block(labels, 2, fake_send, lambda parts: np.concatenate(parts, 0))
    order = np.concatenate(pieces, 0).T
    table = np.empty((LOCAL, SLOTS), np.int32)
    for device in range(LOCAL):
        table[device, order[device]] = np.arange(SLOTS)
    return table


TABLE = piece_table()
PIECES = (16, 8, 8, 16, 16) * 2
STARTS = tuple(int(s) for s in np.cumsum((0,) + PIECES))


def pick_kernel(places, *refs):
    pieces, out, sem = refs[: len(PIECES)], refs[-2], refs[-1]

    def start(i, carry):
        place = places[i]
        for piece, first, last in zip(pieces, STARTS[:-1], STARTS[1:]):

            @pl.when((place >= first) & (place < last))
            def _():
                row = pl.multiple_of((place - first) * STRETCH, STRETCH)
                to = pl.multiple_of(i * STRETCH, STRETCH)
                pltpu.make_async_copy(
                    piece.at[pl.ds(row, STRETCH)], out.at[pl.ds(to, STRETCH)], sem.at[i]
                ).start()

        return carry

    lax.fori_loop(0, TAIL, start, 0)
    for i in range(TAIL):
        rows = pl.ds(i * STRETCH, STRETCH)
        pltpu.make_async_copy(pieces[0].at[pl.ds(0, STRETCH)], out.at[rows], sem.at[i]).wait()


def pick(places, pieces):
    return pl.pallas_call(
        pick_kernel,
        out_shape=jax.ShapeDtypeStruct((TAIL * STRETCH, PAIR), jnp.bfloat16),
        in_specs=[pl.BlockSpec(memory_space=pltpu.SMEM)]
        + [pl.BlockSpec(memory_space=pl.ANY)] * len(pieces),
        out_specs=pl.BlockSpec(memory_space=pl.ANY),
        scratch_shapes=[pltpu.SemaphoreType.DMA((TAIL,))],
        name="pick_tail",
    )(places, *pieces)


def attend_kernel(places, facts, query, grad_out, *refs):
    count = len(PIECES) + 2
    pieces = refs[:count]
    grad_query, block_out, tail_own_out, tail_other_out = refs[count : count + 4]
    rows_in, window, q_heads, g_heads, score, dprob, terms, rows_out, sem, out_sem = refs[count + 4 :]
    scale = 1.0 / HEAD_DIM**0.5
    copies, first = [], 0
    for i, piece in enumerate(pieces):
        rows = piece.shape[0]
        copies.append(pltpu.make_async_copy(piece, rows_in.at[pl.ds(first, rows)], sem.at[i]))
        copies[-1].start()
        first += rows

    def clear(i, carry):
        rows_out[pl.ds(pl.multiple_of(i * 256, 256), 256)] = jnp.zeros((256, PAIR), jnp.bfloat16)
        return carry

    lax.fori_loop(0, rows_out.shape[0] // 256, clear, 0)
    for c in range(2):
        for h in range(HEADS):
            into, rows = pl.ds(h * STRETCH, STRETCH), pl.ds(c * STRETCH, STRETCH)
            columns = pl.ds(h * HEAD_DIM, HEAD_DIM)
            q_heads[c, into] = query[rows, columns]
            g_heads[c, into] = grad_out[rows, columns]
    for copy in copies:
        copy.wait()
    reach = facts[4]
    token = lax.broadcasted_iota(jnp.int32, (1, COLS), 1) % STRETCH
    latest = BACK * STRETCH + token

    def stretch(c, carry):
        def fetch(k, carry):
            place = pl.multiple_of(places[c * KEYS + k] * STRETCH, STRETCH)
            window[pl.ds(pl.multiple_of(k * STRETCH, STRETCH), STRETCH)] = rows_in[pl.ds(place, STRETCH)]
            return carry

        lax.fori_loop(0, KEYS, fetch, 0)
        q, g = q_heads[c], g_heads[c]
        earliest = jnp.maximum(latest - reach, facts[2 + c] * STRETCH)

        def scores(j, peak):
            rows = pl.ds(pl.multiple_of(j * CHUNK, CHUNK), CHUNK)
            keys = window[rows, :HEAD_DIM]
            raw = lax.dot_general(keys, q, (((1,), (1,)), ((), ())), preferred_element_type=jnp.float32)
            row = lax.broadcasted_iota(jnp.int32, (CHUNK, COLS), 0) + j * CHUNK
            seen = (row >= earliest) & (row <= latest)
            raw = jnp.where(seen, raw * (scale * 1.4426950408889634), FAR)
            score[rows] = raw
            return jnp.maximum(peak, jnp.max(raw, axis=0, keepdims=True))

        peak = lax.fori_loop(0, CHUNKS, scores, jnp.full((1, COLS), FAR, jnp.float32))

        def sums(j, carry):
            total, delta = carry
            rows = pl.ds(pl.multiple_of(j * CHUNK, CHUNK), CHUNK)
            expd = jnp.exp2(score[rows] - peak)
            score[rows] = expd
            values = window[rows, HEAD_DIM:]
            dp = lax.dot_general(values, g, (((1,), (1,)), ((), ())), preferred_element_type=jnp.float32)
            dprob[rows] = dp
            total = total + jnp.sum(expd, axis=0, keepdims=True)
            delta = delta + jnp.sum(expd * dp, axis=0, keepdims=True)
            return total, delta

        zero = jnp.zeros((1, COLS), jnp.float32)
        total, delta = lax.fori_loop(0, CHUNKS, sums, (zero, zero))
        share = 1.0 / total
        delta = delta * share

        def grads(j, dq):
            rows = pl.ds(pl.multiple_of(j * CHUNK, CHUNK), CHUNK)
            prob = score[rows] * share
            dscore = (prob * (dprob[rows] - delta)).astype(jnp.bfloat16)
            terms[c, rows, HEAD_DIM:] = jnp.dot(
                prob.astype(jnp.bfloat16), g, preferred_element_type=jnp.float32
            )
            terms[c, rows, :HEAD_DIM] = jnp.dot(dscore, q, preferred_element_type=jnp.float32) * scale
            keys = window[rows, :HEAD_DIM]
            return dq + lax.dot_general(
                keys, dscore, (((0,), (0,)), ((), ())), preferred_element_type=jnp.float32
            )

        dq = lax.fori_loop(0, CHUNKS, grads, jnp.zeros((HEAD_DIM, COLS), jnp.float32))
        dq = (jnp.transpose(dq) * scale).astype(jnp.bfloat16)
        for h in range(HEADS):
            grad_query[pl.ds(pl.multiple_of(c * STRETCH, STRETCH), STRETCH), pl.ds(h * HEAD_DIM, HEAD_DIM)] = dq[
                h * STRETCH : (h + 1) * STRETCH
            ]
        return carry

    lax.fori_loop(0, 2, stretch, 0)

    def place_first(k, carry):
        @pl.when(k >= facts[2])
        def _():
            place = pl.multiple_of(places[k] * STRETCH, STRETCH)
            rows = pl.ds(pl.multiple_of(k * STRETCH, STRETCH), STRETCH)
            rows_out[pl.ds(place, STRETCH)] = terms[0, rows].astype(jnp.bfloat16)

        return carry

    lax.fori_loop(0, KEYS, place_first, 0)

    def place_second(k, carry):
        @pl.when(k >= facts[3])
        def _():
            place = pl.multiple_of(places[KEYS + k] * STRETCH, STRETCH)
            rows = pl.ds(pl.multiple_of(k * STRETCH, STRETCH), STRETCH)
            twin = k + facts[1] - facts[0]
            both = (twin >= facts[2]) & (twin < KEYS)
            twin = jnp.clip(twin, 0, KEYS - 1)
            first = terms[0, pl.ds(pl.multiple_of(twin * STRETCH, STRETCH), STRETCH)]
            term = terms[1, rows] + jnp.where(both, first, 0.0)
            rows_out[pl.ds(place, STRETCH)] = term.astype(jnp.bfloat16)

        return carry

    lax.fori_loop(0, KEYS, place_second, 0)
    copies, first = [], 0
    for i, out in enumerate((block_out, tail_own_out, tail_other_out)):
        rows = out.shape[0]
        copies.append(pltpu.make_async_copy(rows_out.at[pl.ds(first, rows)], out, out_sem.at[i]))
        copies[-1].start()
        first += rows
    for copy in copies:
        copy.wait()


def attend(places, facts, query, grad_out, pieces):
    rows = (SLOTS + BACK) * STRETCH
    tail = TAIL * STRETCH
    shape = jax.ShapeDtypeStruct
    smem = pl.BlockSpec(memory_space=pltpu.SMEM)
    vmem = pl.BlockSpec(memory_space=pltpu.VMEM)
    anywhere = pl.BlockSpec(memory_space=pl.ANY)
    return pl.pallas_call(
        attend_kernel,
        out_shape=(
            shape(query.shape, jnp.bfloat16),
            shape((SLOTS * STRETCH, PAIR), jnp.bfloat16),
            shape((tail, PAIR), jnp.bfloat16),
            shape((tail, PAIR), jnp.bfloat16),
        ),
        in_specs=[smem, smem, vmem, vmem] + [anywhere] * len(pieces),
        out_specs=(vmem, anywhere, anywhere, anywhere),
        scratch_shapes=[
            pltpu.VMEM((rows, PAIR), jnp.bfloat16),
            pltpu.VMEM((WINDOW, PAIR), jnp.bfloat16),
            pltpu.VMEM((2, COLS, HEAD_DIM), jnp.bfloat16),
            pltpu.VMEM((2, COLS, HEAD_DIM), jnp.bfloat16),
            pltpu.VMEM((WINDOW, COLS), jnp.float32),
            pltpu.VMEM((WINDOW, COLS), jnp.float32),
            pltpu.VMEM((2, WINDOW, PAIR), jnp.float32),
            pltpu.VMEM((rows, PAIR), jnp.bfloat16),
            pltpu.SemaphoreType.DMA((len(pieces),)),
            pltpu.SemaphoreType.DMA((3,)),
        ],
        compiler_params=pltpu.CompilerParams(vmem_limit_bytes=40 * 2**20),
        name="attend",
    )(places, facts, query, grad_out, *pieces)


def merge_kernel(places, block, tail, *refs):
    outs, held, sem, out_sem = refs[: len(PIECES)], refs[-3], refs[-2], refs[-1]
    copy = pltpu.make_async_copy(block, held, sem.at[0])
    copy.start()
    copy.wait()

    def add(i, carry):
        rows = pl.ds(pl.multiple_of(places[i] * STRETCH, STRETCH), STRETCH)
        term = tail[pl.ds(pl.multiple_of(i * STRETCH, STRETCH), STRETCH)]
        held[rows] = (held[rows].astype(jnp.float32) + term.astype(jnp.float32)).astype(jnp.bfloat16)
        return carry

    lax.fori_loop(0, TAIL, add, 0)
    copies = []
    for i, out in enumerate(outs):
        rows = pl.ds(STARTS[i] * STRETCH, PIECES[i] * STRETCH)
        copies.append(pltpu.make_async_copy(held.at[rows], out, out_sem.at[i]))
        copies[-1].start()
    for copy in copies:
        copy.wait()


def merge(places, block, tail):
    anywhere = pl.BlockSpec(memory_space=pl.ANY)
    return pl.pallas_call(
        merge_kernel,
        out_shape=tuple(jax.ShapeDtypeStruct((n * STRETCH, PAIR), jnp.bfloat16) for n in PIECES),
        in_specs=[pl.BlockSpec(memory_space=pltpu.SMEM), anywhere, pl.BlockSpec(memory_space=pltpu.VMEM)],
        out_specs=(anywhere,) * len(PIECES),
        scratch_shapes=[
            pltpu.VMEM(block.shape, jnp.bfloat16),
            pltpu.SemaphoreType.DMA((1,)),
            pltpu.SemaphoreType.DMA((len(PIECES),)),
        ],
        compiler_params=pltpu.CompilerParams(vmem_limit_bytes=16 * 2**20),
        name="merge_tail",
    )(places, block, tail)


def wide(value):
    return value.astype(jnp.float32)


def reduce_block(pieces, unit):
    own, other = pieces[:5], pieces[5:]
    arrived = [swap(piece) for piece in other]
    sums = [wide(a) + wide(b) for a, b in zip(own, arrived)]
    mine, up, down, ahead, behind = [sums[0]] + [s.astype(jnp.bfloat16) for s in sums[1:]]
    ahead, behind = shift(ahead, -1, 0), shift(behind, 1, 0)
    up, down = shift(up, 0, -1), shift(down, 0, 1)
    half = up.shape[0]
    mine = mine + wide(ahead) + wide(behind)
    mine = jnp.concatenate([mine[:half] + wide(up) + wide(down), mine[half:]], 0)
    mine_b = mine.astype(jnp.bfloat16)
    back = []
    for i, by_core in enumerate(MEMBERS):
        rows = mine_b[(2 + 2 * i) * unit : (4 + 2 * i) * unit]
        back.append(send(rows, tuple((-dz, -dy) for dz, dy in by_core)))
    opposite = shift(mine_b[unit : 2 * unit], -OPPOSITE[0], -OPPOSITE[1])
    there = sum(wide(b[unit:]) for b in back)
    here = mine[:unit] + wide(opposite) + sum(wide(b[:unit]) for b in back)
    return here + wide(swap(there.astype(jnp.bfloat16)))


def per_device(query, key, value, grad_out, stretch_order, reach):
    unit = query.shape[0]
    node, local = lax.axis_index("node"), lax.axis_index("local")
    core = local % 2
    order = lax.dynamic_index_in_dim(stretch_order, node, 0, keepdims=False)
    table = lax.dynamic_index_in_dim(jnp.asarray(TABLE), local, 0, keepdims=False)
    own = lax.dynamic_slice_in_dim(order, 2 * local, 2)

    def find(wanted):
        match = order[None, :] == wanted[:, None]
        return jnp.sum(jnp.where(match, table[None, :], 0), axis=1)

    wanted = (own[:, None] - BACK + jnp.arange(KEYS, dtype=jnp.int32)[None, :]).reshape(-1)
    tail = wanted + BACK
    in_tail = SLOTS + jnp.where(tail // TAIL == core, 0, TAIL) + tail % TAIL
    places = jnp.where(wanted >= 0, find(wanted), jnp.where(node > 0, in_tail, 0))
    tail_places = find(SLOTS - BACK + core * TAIL + jnp.arange(TAIL, dtype=jnp.int32))
    first_seen = jnp.where(node > 0, 0, jnp.maximum(BACK - own, 0))
    own_reach = lax.dynamic_slice_in_dim(reach, node, 1)
    facts = jnp.concatenate([own, first_seen, own_reach]).astype(jnp.int32)

    pair = jnp.concatenate([key, value], axis=1)
    pieces = gather_block(pair, unit, send, lambda parts: jnp.concatenate(parts, 0))
    nodes = lax.axis_size("node")
    tail_own = lax.ppermute(pick(tail_places, pieces), "node", [(n, n + 1) for n in range(nodes - 1)])
    tail_other = swap(tail_own)
    grad_query, block, back_own, back_other = attend(
        places, facts, query, grad_out, pieces + [tail_own, tail_other]
    )
    back = (wide(back_own) + wide(swap(back_other))).astype(jnp.bfloat16)
    back = lax.ppermute(back, "node", [(n + 1, n) for n in range(nodes - 1)])
    sums = reduce_block(merge(tail_places, block, back), unit).astype(jnp.bfloat16)
    return grad_query, sums[:, :HEAD_DIM], sums[:, HEAD_DIM:]


def solution(mesh):
    rows = P(("node", "local"), None)
    return jax.shard_map(
        per_device,
        mesh=mesh,
        in_specs=(rows, rows, rows, rows, P(), P()),
        out_specs=(rows, rows, rows),
        check_vma=False,
    )
```

```python
import functools

import jax
import jax.numpy as jnp
import numpy as np
from jax import lax
from jax.experimental import pallas as pl
from jax.experimental.pallas import tpu as pltpu
from jax.sharding import PartitionSpec as P

HEAD_DIM = 128
HEADS = 8
STRETCH = 64
SLOTS = 128
BACK = 32
KEYS = BACK + 1
WINDOW = KEYS * STRETCH
COLS = HEADS * STRETCH
CHUNK = 11 * STRETCH
CHUNKS = WINDOW // CHUNK
TAIL = BACK // 2
NZ, NY = 8, 4
LOCAL = NZ * NY * 2
FAR = -1e30

MEMBERS = (((2, 1), (6, 1)), ((6, 3), (2, 3)), ((0, 2), (4, 0)))
OPPOSITE = (4, 2)


def local_of(z, y, c):
    return ((z % NZ) * NY + y % NY) * 2 + c


def moves(by_core):
    out = []
    for source in range(LOCAL):
        z, y, c = source // (NY * 2), (source // 2) % NY, source % 2
        if by_core is None:
            out.append((source, local_of(z, y, 1 - c)))
        else:
            dz, dy = by_core[c]
            out.append((source, local_of(z + dz, y + dy, c)))
    return out


def send(value, by_core):
    return lax.ppermute(value, "local", moves(by_core))


def swap(value):
    return send(value, None)


def shift(value, dz, dy):
    return send(value, ((dz, dy), (dz, dy)))


def gather_block(own, unit, send, join, settle=lambda early, late: late):
    swap = functools.partial(send, by_core=None)
    chip = join([own, swap(own)])
    members = [send(chip, by_core=m) for m in MEMBERS]
    opposite = send(own, by_core=(OPPOSITE, OPPOSITE))
    mine = join([own, settle(members[0], opposite)] + members)
    half = 4 * unit
    up = send(mine[:half], by_core=((0, 1), (0, 1)))
    down = send(mine[:half], by_core=((0, -1), (0, -1)))
    ahead = send(mine, by_core=((1, 0), (1, 0)))
    behind = send(mine, by_core=((-1, 0), (-1, 0)))
    pieces = [mine, up, down, ahead, behind]
    return pieces + [swap(piece) for piece in pieces]


def piece_table():
    labels = np.arange(SLOTS).reshape(LOCAL, 2).T

    def fake_send(value, by_core):
        out = np.empty_like(value)
        for source, target in moves(by_core):
            out[:, target] = value[:, source]
        return out

    pieces = gather_block(labels, 2, fake_send, lambda parts: np.concatenate(parts, 0))
    order = np.concatenate(pieces, 0).T
    table = np.empty((LOCAL, SLOTS), np.int32)
    for device in range(LOCAL):
        table[device, order[device]] = np.arange(SLOTS)
    return table


TABLE = piece_table()
PIECES = (16, 8, 8, 16, 16) * 2
ALL = PIECES + (TAIL, TAIL)
STARTS = tuple(int(s) for s in np.cumsum((0,) + ALL))
KEY_COST = 0
VALUE_COST = 6
VMEM_LIMIT = 36 * 2**20
PICK_KIB = 12 * 1024
MERGE_KIB = 16 * 1024

SMEM = pl.BlockSpec(memory_space=pltpu.SMEM)
VMEM = pl.BlockSpec(memory_space=pltpu.VMEM)


def at(i, size=STRETCH):
    return pl.ds(pl.multiple_of(i * size, size), size)


def shape(rows, columns=HEAD_DIM, dtype=jnp.bfloat16):
    return jax.ShapeDtypeStruct((rows, columns), dtype)


def lay(refs, held, columns=slice(None)):
    first = 0
    for ref in refs:
        held[pl.ds(first, ref.shape[0])] = ref[:, columns]
        first += ref.shape[0]


def small(kib):
    return pltpu.CompilerParams(vmem_limit_bytes=kib * 1024)


def plan_kernel(order, reach, table, places, tail_places, facts, inverse):
    node, local = lax.axis_index("node"), lax.axis_index("local")
    core = local % 2

    def turn(s, carry):
        inverse[order[node, s]] = table[local, s]
        return carry

    lax.fori_loop(0, SLOTS, turn, 0, unroll=8)
    for i in range(TAIL):
        tail_places[i] = inverse[SLOTS - BACK + core * TAIL + i]
    facts[4] = reach[node]
    for c in range(2):
        own = order[node, 2 * local + c]
        facts[c] = own
        first = jnp.where(node > 0, 0, jnp.maximum(BACK - own, 0))
        facts[2 + c] = first

        def find(k, carry, c=c, own=own):
            wanted = own - BACK + k
            tail = jnp.maximum(wanted + BACK, 0)
            half = tail // TAIL
            in_tail = SLOTS + jnp.where(half == core, 0, TAIL) + tail % TAIL
            now = inverse[jnp.maximum(wanted, 0)]
            places[c * KEYS + k] = jnp.where(wanted >= 0, now, jnp.where(node > 0, in_tail, 0))
            return carry

        lax.fori_loop(0, KEYS, find, 0, unroll=3)


def plan(stretch_order, reach):
    return pl.pallas_call(
        plan_kernel,
        out_shape=tuple(jax.ShapeDtypeStruct((n,), jnp.int32) for n in (2 * KEYS, TAIL, 5)),
        in_specs=[SMEM] * 3,
        out_specs=(SMEM,) * 3,
        scratch_shapes=[pltpu.SMEM((SLOTS,), jnp.int32)],
        compiler_params=small(256),
        name="plan",
    )(stretch_order, reach, jnp.asarray(TABLE))


def pick_kernel(places, *refs):
    pieces, keys, values, held = refs[: len(PIECES)], *refs[len(PIECES) :]
    lay(pieces, held)

    def one(i, carry):
        rows = held[at(places[i])]
        keys[at(i)], values[at(i)] = rows[:, :HEAD_DIM], rows[:, HEAD_DIM:]
        return carry

    lax.fori_loop(0, TAIL, one, 0)


def pick(places, pieces):
    return pl.pallas_call(
        pick_kernel,
        out_shape=(shape(TAIL * STRETCH),) * 2,
        in_specs=[SMEM] + [VMEM] * len(pieces),
        out_specs=(VMEM,) * 2,
        scratch_shapes=[pltpu.VMEM((SLOTS * STRETCH, 2 * HEAD_DIM), jnp.bfloat16)],
        compiler_params=small(PICK_KIB),
        name="pick_tail",
    )(places, *pieces)


def stack_heads(array, heads):
    for c in range(2):
        for h in range(HEADS):
            heads[c, pl.ds(h * STRETCH, STRETCH)] = array[
                pl.ds(c * STRETCH, STRETCH), pl.ds(h * HEAD_DIM, HEAD_DIM)
            ]


def fetch(places, c, held, window):
    def one(k, carry):
        window[at(k)] = held[at(places[c * KEYS + k])]
        return carry

    lax.fori_loop(0, KEYS, one, 0, unroll=11)


def spread(places, facts, terms, held):
    def clear(i, carry):
        held[at(i, 256)] = jnp.zeros((256, HEAD_DIM), jnp.bfloat16)
        return carry

    lax.fori_loop(0, held.shape[0] // 256, clear, 0, unroll=8)

    dump = SLOTS + BACK

    def first(k, carry):
        place = jnp.where(k >= facts[2], places[k], dump)
        held[at(place)] = terms[0, at(k)].astype(jnp.bfloat16)
        return carry

    lax.fori_loop(0, KEYS, first, 0, unroll=11)

    def second(k, carry):
        place = jnp.where(k >= facts[3], places[KEYS + k], dump)
        twin = k + facts[1] - facts[0]
        both = (twin >= facts[2]) & (twin < KEYS)
        twin = jnp.clip(twin, 0, KEYS - 1)
        term = terms[1, at(k)] + jnp.where(both, terms[0, at(twin)], 0.0)
        held[at(place)] = term.astype(jnp.bfloat16)
        return carry

    lax.fori_loop(0, KEYS, second, 0, unroll=11)


def give(held, outs):
    first = 0
    for out in outs:
        out[...] = held[pl.ds(first, out.shape[0])]
        first += out.shape[0]


def dot(a, b, over):
    return lax.dot_general(a, b, ((over[:1], over[1:]), ((), ())), preferred_element_type=jnp.float32)


def key_kernel(places, facts, query, grad_out, *refs):
    pieces, refs = refs[: len(ALL)], refs[len(ALL) :]
    prob_out, keys_out, q_heads, g_heads, *outs = refs[:7]
    held, score, terms = refs[7:]
    lay(pieces, held, pl.ds(0, HEAD_DIM))
    scale = 1.4426950408889634 / HEAD_DIM**0.5
    stack_heads(query, q_heads)
    stack_heads(grad_out, g_heads)
    token = lax.broadcasted_iota(jnp.int32, (1, COLS), 1) % STRETCH
    latest = BACK * STRETCH + token

    for c in range(2):
        window = keys_out.at[c]
        fetch(places, c, held, window)
        q, g = q_heads[c], g_heads[c]
        earliest = jnp.maximum(latest - facts[4], facts[2 + c] * STRETCH)
        peaks, totals = [], []
        for j in range(CHUNKS):
            rows = pl.ds(j * CHUNK, CHUNK)
            raw = dot(window[rows], q, (1, 1))
            row = lax.broadcasted_iota(jnp.int32, (CHUNK, COLS), 0) + j * CHUNK
            seen = row >= earliest
            if (j + 1) * CHUNK > BACK * STRETCH:
                seen = seen & (row <= latest)
            raw = jnp.where(seen, raw * scale, FAR)
            score[c, rows] = raw
            peaks.append(jnp.max(raw, axis=0, keepdims=True))
            expd = jnp.exp2(score[c, rows] - peaks[j])
            score[c, rows] = expd
            totals.append(jnp.sum(expd, axis=0, keepdims=True))
        peak = functools.reduce(jnp.maximum, peaks)
        weights = [jnp.exp2(p - peak) for p in peaks]
        share = 1.0 / sum(w * t for w, t in zip(weights, totals))
        for j in range(CHUNKS):
            rows = pl.ds(j * CHUNK, CHUNK)
            prob = (score[c, rows] * (share * weights[j])).astype(jnp.bfloat16)
            prob_out[c, rows] = prob
            terms[c, rows] = dot(prob, g, (1, 0))
    spread(places, facts, terms, held)
    give(held, outs)


def value_kernel(places, facts, prob_in, keys_in, q_heads, g_heads, *refs):
    pieces, refs = refs[: len(ALL)], refs[len(ALL) :]
    grad_query, *outs = refs[:4]
    held, window, dprob, terms = refs[4:]
    lay(pieces[: len(PIECES)], held, pl.ds(HEAD_DIM, HEAD_DIM))
    lay(pieces[len(PIECES) :], held.at[pl.ds(SLOTS * STRETCH, 2 * TAIL * STRETCH)])
    scale = 1.0 / HEAD_DIM**0.5

    for c in range(2):
        fetch(places, c, held, window.at[c])
        q, g = q_heads[c], g_heads[c]
        delta = 0.0
        for j in range(CHUNKS):
            rows = pl.ds(j * CHUNK, CHUNK)
            dp = dot(window[c, rows], g, (1, 1))
            dprob[c, rows] = dp
            delta = delta + jnp.sum(prob_in[c, rows].astype(jnp.float32) * dp, axis=0, keepdims=True)
        dq = 0.0
        for j in range(CHUNKS):
            rows = pl.ds(j * CHUNK, CHUNK)
            prob = prob_in[c, rows].astype(jnp.float32)
            dscore = (prob * (dprob[c, rows] - delta)).astype(jnp.bfloat16)
            terms[c, rows] = dot(dscore, q, (1, 0)) * scale
            dq = dq + dot(keys_in[c, rows], dscore, (0, 0))
        dq = (jnp.transpose(dq) * scale).astype(jnp.bfloat16)
        for h in range(HEADS):
            grad_query[pl.ds(c * STRETCH, STRETCH), pl.ds(h * HEAD_DIM, HEAD_DIM)] = dq[
                h * STRETCH : (h + 1) * STRETCH
            ]
    spread(places, facts, terms, held)
    give(held, outs)


PIECE_SHAPES = tuple(shape(n * STRETCH, 2 * HEAD_DIM) for n in PIECES)
TERM_SHAPES = (shape(SLOTS * STRETCH), shape(TAIL * STRETCH), shape(TAIL * STRETCH))
HEAD_SHAPE = jax.ShapeDtypeStruct((2, COLS, HEAD_DIM), jnp.bfloat16)


def cost(matmuls):
    return pl.CostEstimate(
        flops=matmuls * 4 * WINDOW * COLS * HEAD_DIM, bytes_accessed=matmuls * 2**21, transcendentals=0
    )


def on_keys(places, facts, query, grad_out, pieces):
    return pl.pallas_call(
        key_kernel,
        out_shape=(
            jax.ShapeDtypeStruct((2, WINDOW, COLS), jnp.bfloat16),
            jax.ShapeDtypeStruct((2, WINDOW, HEAD_DIM), jnp.bfloat16),
            HEAD_SHAPE,
            HEAD_SHAPE,
        )
        + TERM_SHAPES,
        in_specs=[SMEM, SMEM] + [VMEM] * (2 + len(pieces)),
        out_specs=(VMEM,) * 7,
        scratch_shapes=[
            pltpu.VMEM(((SLOTS + BACK + 1) * STRETCH, HEAD_DIM), jnp.bfloat16),
            pltpu.VMEM((2, WINDOW, COLS), jnp.float32),
            pltpu.VMEM((2, WINDOW, HEAD_DIM), jnp.float32),
        ],
        compiler_params=pltpu.CompilerParams(vmem_limit_bytes=VMEM_LIMIT),
        cost_estimate=cost(KEY_COST),
        name="on_keys",
    )(places, facts, query, grad_out, *pieces)


def on_values(places, facts, carried, pieces):
    return pl.pallas_call(
        value_kernel,
        out_shape=(shape(2 * STRETCH, HEADS * HEAD_DIM),) + TERM_SHAPES,
        in_specs=[SMEM, SMEM] + [VMEM] * (4 + len(pieces)),
        out_specs=(VMEM,) * 4,
        scratch_shapes=[
            pltpu.VMEM(((SLOTS + BACK + 1) * STRETCH, HEAD_DIM), jnp.bfloat16),
            pltpu.VMEM((2, WINDOW, HEAD_DIM), jnp.bfloat16),
            pltpu.VMEM((2, WINDOW, COLS), jnp.float32),
            pltpu.VMEM((2, WINDOW, HEAD_DIM), jnp.float32),
        ],
        compiler_params=pltpu.CompilerParams(vmem_limit_bytes=VMEM_LIMIT),
        cost_estimate=cost(VALUE_COST),
        name="on_values",
    )(places, facts, *carried, *pieces)


def merge_kernel(places, keys, values, tail_keys, tail_values, *refs):
    outs, held = refs[:-1], refs[-1]
    for i, (block, tail) in enumerate(((keys, tail_keys), (values, tail_values))):
        columns = pl.ds(i * HEAD_DIM, HEAD_DIM)
        held[:, columns] = block[...]

        def one(j, carry, tail=tail, columns=columns):
            rows = at(places[j])
            total = held[rows, columns].astype(jnp.float32) + tail[at(j)].astype(jnp.float32)
            held[rows, columns] = total.astype(jnp.bfloat16)
            return carry

        lax.fori_loop(0, TAIL, one, 0)
    give(held, outs)


def merge(places, *arrays):
    return pl.pallas_call(
        merge_kernel,
        out_shape=PIECE_SHAPES,
        in_specs=[SMEM] + [VMEM] * len(arrays),
        out_specs=(VMEM,) * len(PIECES),
        scratch_shapes=[pltpu.VMEM((SLOTS * STRETCH, 2 * HEAD_DIM), jnp.bfloat16)],
        compiler_params=small(MERGE_KIB),
        name="merge_tail",
    )(places, *arrays)


def join(parts):
    return jnp.concatenate(parts, 0)


def wide(value):
    return value.astype(jnp.float32)


def reduce_block(pieces, unit):
    own, other = pieces[:5], pieces[5:]
    arrived = [swap(piece) for piece in other]
    sums = [wide(a) + wide(b) for a, b in zip(own, arrived)]
    mine, up, down, ahead, behind = [sums[0]] + [s.astype(jnp.bfloat16) for s in sums[1:]]
    ahead, behind = shift(ahead, -1, 0), shift(behind, 1, 0)
    up, down = shift(up, 0, -1), shift(down, 0, 1)
    half = up.shape[0]
    mine = mine + wide(ahead) + wide(behind)
    mine = jnp.concatenate([mine[:half] + wide(up) + wide(down), mine[half:]], 0)
    mine_b = mine.astype(jnp.bfloat16)
    back = []
    for i, by_core in enumerate(MEMBERS):
        rows = mine_b[(2 + 2 * i) * unit : (4 + 2 * i) * unit]
        back.append(send(rows, tuple((-dz, -dy) for dz, dy in by_core)))
    opposite = shift(mine_b[unit : 2 * unit], -OPPOSITE[0], -OPPOSITE[1])
    there = sum(wide(b[unit:]) for b in back)
    here = mine[:unit] + wide(opposite) + sum(wide(b[:unit]) for b in back)
    return here + wide(swap(there.astype(jnp.bfloat16)))


def join(parts):
    return jnp.concatenate(parts, 0)


def per_device(query, key, value, grad_out, stretch_order, reach):
    unit = query.shape[0]
    nodes = lax.axis_size("node")
    onward = [(n, (n + 1) % nodes) for n in range(nodes)]
    backward = [((n + 1) % nodes, n) for n in range(nodes)]
    tables = []

    def settle(early, late):
        tables.extend(plan(stretch_order, lax.optimization_barrier((reach, early))[0]))
        late, *tables[:] = lax.optimization_barrier((late, *tables))
        return late

    pieces = gather_block(jnp.concatenate([key, value], axis=1), unit, send, join, settle)
    places, tail_places, facts = tables
    tails = [lax.ppermute(tail, "node", onward) for tail in pick(tail_places, pieces)]
    keys, values = [pieces + [tail, swap(tail)] for tail in tails]

    *carried, block_values, own_tail, other_tail = on_keys(places, facts, query, grad_out, keys)
    tail_values = (wide(own_tail) + wide(swap(other_tail))).astype(jnp.bfloat16)
    carried[0], tail_values = lax.optimization_barrier((carried[0], tail_values))
    tail_values = lax.ppermute(tail_values, "node", backward)
    grad_query, block_keys, own_tail, other_tail = on_values(places, facts, carried, values)
    tail_values, own_tail, other_tail = lax.optimization_barrier((tail_values, own_tail, other_tail))
    tail_keys = (wide(own_tail) + wide(swap(other_tail))).astype(jnp.bfloat16)
    tail_keys = lax.ppermute(tail_keys, "node", backward)
    pieces = merge(tail_places, block_keys, block_values, tail_keys, tail_values)
    sums = reduce_block(pieces, unit).astype(jnp.bfloat16)
    return grad_query, sums[:, :HEAD_DIM], sums[:, HEAD_DIM:]


def solution(mesh):
    rows = P(("node", "local"), None)
    return jax.shard_map(
        per_device,
        mesh=mesh,
        in_specs=(rows, rows, rows, rows, P(), P()),
        out_specs=(rows, rows, rows),
        check_vma=False,
    )
```

```python
import functools

import jax
import jax.numpy as jnp
import numpy as np
from jax import lax
from jax.experimental import pallas as pl
from jax.experimental.pallas import tpu as pltpu
from jax.sharding import PartitionSpec as P

HEAD_DIM = 128
HEADS = 8
STRETCH = 64
SLOTS = 128
BACK = 32
KEYS = BACK + 1
WINDOW = KEYS * STRETCH
COLS = HEADS * STRETCH
CHUNK = 11 * STRETCH
CHUNKS = WINDOW // CHUNK
TAIL = BACK // 2
NZ, NY = 8, 4
LOCAL = NZ * NY * 2
FAR = -1e30

MEMBERS = (((2, 0), (6, 0)), ((1, 2), (5, 2)), ((3, 2), (7, 2)))


def local_of(z, y, c):
    return ((z % NZ) * NY + y % NY) * 2 + c


def moves(by_core):
    out = []
    for source in range(LOCAL):
        z, y, c = source // (NY * 2), (source // 2) % NY, source % 2
        if by_core is None:
            out.append((source, local_of(z, y, 1 - c)))
        else:
            dz, dy = by_core[c]
            out.append((source, local_of(z + dz, y + dy, c)))
    return out


def send(value, by_core):
    return lax.ppermute(value, "local", moves(by_core))


def swap(value):
    return send(value, None)


def shift(value, dz, dy):
    return send(value, ((dz, dy), (dz, dy)))


def gather_block(own, unit, send, join, settle=lambda early, late: late):
    swap = functools.partial(send, by_core=None)
    chip = join([own, swap(own)])
    first, second, third = [send(chip, by_core=m) for m in MEMBERS]
    opposite = send(first[:unit], by_core=MEMBERS[0])
    mine = join([own, second, settle(first, opposite), first, third])
    half = 4 * unit
    up, down = [send(mine, by_core=((0, dy), (0, dy))) for dy in (1, -1)]
    ahead, behind = [send(mine[:half], by_core=((dz, 0), (dz, 0))) for dz in (1, -1)]
    pieces = [mine, up, down, ahead, behind]
    return pieces + [swap(piece) for piece in pieces]


def piece_table():
    labels = np.arange(SLOTS).reshape(LOCAL, 2).T

    def fake_send(value, by_core):
        out = np.empty_like(value)
        for source, target in moves(by_core):
            out[:, target] = value[:, source]
        return out

    pieces = gather_block(labels, 2, fake_send, lambda parts: np.concatenate(parts, 0))
    order = np.concatenate(pieces, 0).T
    table = np.empty((LOCAL, SLOTS), np.int32)
    for device in range(LOCAL):
        table[device, order[device]] = np.arange(SLOTS)
    return table


TABLE = piece_table()
PIECES = (16, 16, 16, 8, 8) * 2
ALL = PIECES + (TAIL, TAIL)
STARTS = tuple(int(s) for s in np.cumsum((0,) + ALL))
KEY_COST = 0
VALUE_COST = 6
VMEM_LIMIT = 36 * 2**20
PICK_KIB = 12 * 1024
MERGE_KIB = 16 * 1024

SMEM = pl.BlockSpec(memory_space=pltpu.SMEM)
VMEM = pl.BlockSpec(memory_space=pltpu.VMEM)


def at(i, size=STRETCH):
    return pl.ds(pl.multiple_of(i * size, size), size)


def shape(rows, columns=HEAD_DIM, dtype=jnp.bfloat16):
    return jax.ShapeDtypeStruct((rows, columns), dtype)


def lay(refs, held, columns=slice(None)):
    first = 0
    for ref in refs:
        held[pl.ds(first, ref.shape[0])] = ref[:, columns]
        first += ref.shape[0]


def small(kib):
    return pltpu.CompilerParams(vmem_limit_bytes=kib * 1024)


def plan_kernel(order, reach, table, places, tail_places, facts, inverse):
    node, local = lax.axis_index("node"), lax.axis_index("local")
    core = local % 2

    def turn(s, carry):
        inverse[order[node, s]] = table[local, s]
        return carry

    lax.fori_loop(0, SLOTS, turn, 0, unroll=8)
    for i in range(TAIL):
        tail_places[i] = inverse[SLOTS - BACK + core * TAIL + i]
    facts[4] = reach[node]
    for c in range(2):
        own = order[node, 2 * local + c]
        facts[c] = own
        first = jnp.where(node > 0, 0, jnp.maximum(BACK - own, 0))
        facts[2 + c] = first

        def find(k, carry, c=c, own=own):
            wanted = own - BACK + k
            tail = jnp.maximum(wanted + BACK, 0)
            half = tail // TAIL
            in_tail = SLOTS + jnp.where(half == core, 0, TAIL) + tail % TAIL
            now = inverse[jnp.maximum(wanted, 0)]
            places[c * KEYS + k] = jnp.where(wanted >= 0, now, jnp.where(node > 0, in_tail, 0))
            return carry

        lax.fori_loop(0, KEYS, find, 0, unroll=3)


def plan(stretch_order, reach):
    return pl.pallas_call(
        plan_kernel,
        out_shape=tuple(jax.ShapeDtypeStruct((n,), jnp.int32) for n in (2 * KEYS, TAIL, 5)),
        in_specs=[SMEM] * 3,
        out_specs=(SMEM,) * 3,
        scratch_shapes=[pltpu.SMEM((SLOTS,), jnp.int32)],
        compiler_params=small(256),
        name="plan",
    )(stretch_order, reach, jnp.asarray(TABLE))


def pick_kernel(places, *refs):
    pieces, keys, values, held = refs[: len(PIECES)], *refs[len(PIECES) :]
    lay(pieces, held)

    def one(i, carry):
        rows = held[at(places[i])]
        keys[at(i)], values[at(i)] = rows[:, :HEAD_DIM], rows[:, HEAD_DIM:]
        return carry

    lax.fori_loop(0, TAIL, one, 0)


def pick(places, pieces):
    return pl.pallas_call(
        pick_kernel,
        out_shape=(shape(TAIL * STRETCH),) * 2,
        in_specs=[SMEM] + [VMEM] * len(pieces),
        out_specs=(VMEM,) * 2,
        scratch_shapes=[pltpu.VMEM((SLOTS * STRETCH, 2 * HEAD_DIM), jnp.bfloat16)],
        compiler_params=small(PICK_KIB),
        name="pick_tail",
    )(places, *pieces)


def stack_heads(array, heads):
    for c in range(2):
        for h in range(HEADS):
            heads[c, pl.ds(h * STRETCH, STRETCH)] = array[
                pl.ds(c * STRETCH, STRETCH), pl.ds(h * HEAD_DIM, HEAD_DIM)
            ]


def fetch(places, c, held, window):
    def one(k, carry):
        window[at(k)] = held[at(places[c * KEYS + k])]
        return carry

    lax.fori_loop(0, KEYS, one, 0, unroll=11)


def spread(places, facts, terms, held):
    def clear(i, carry):
        held[at(i, 256)] = jnp.zeros((256, HEAD_DIM), jnp.bfloat16)
        return carry

    lax.fori_loop(0, held.shape[0] // 256, clear, 0, unroll=8)

    dump = SLOTS + BACK

    def first(k, carry):
        place = jnp.where(k >= facts[2], places[k], dump)
        held[at(place)] = terms[0, at(k)].astype(jnp.bfloat16)
        return carry

    lax.fori_loop(0, KEYS, first, 0, unroll=11)

    def second(k, carry):
        place = jnp.where(k >= facts[3], places[KEYS + k], dump)
        twin = k + facts[1] - facts[0]
        both = (twin >= facts[2]) & (twin < KEYS)
        twin = jnp.clip(twin, 0, KEYS - 1)
        term = terms[1, at(k)] + jnp.where(both, terms[0, at(twin)], 0.0)
        held[at(place)] = term.astype(jnp.bfloat16)
        return carry

    lax.fori_loop(0, KEYS, second, 0, unroll=11)


def give(held, outs):
    first = 0
    for out in outs:
        out[...] = held[pl.ds(first, out.shape[0])]
        first += out.shape[0]


def dot(a, b, over):
    return lax.dot_general(a, b, ((over[:1], over[1:]), ((), ())), preferred_element_type=jnp.float32)


def key_kernel(places, facts, query, grad_out, *refs):
    pieces, refs = refs[: len(ALL)], refs[len(ALL) :]
    prob_out, keys_out, q_heads, g_heads, *outs = refs[:7]
    held, score, terms = refs[7:]
    lay(pieces, held, pl.ds(0, HEAD_DIM))
    scale = 1.4426950408889634 / HEAD_DIM**0.5
    stack_heads(query, q_heads)
    stack_heads(grad_out, g_heads)
    token = lax.broadcasted_iota(jnp.int32, (1, COLS), 1) % STRETCH
    latest = BACK * STRETCH + token

    for c in range(2):
        window = keys_out.at[c]
        fetch(places, c, held, window)
        q, g = q_heads[c], g_heads[c]
        earliest = jnp.maximum(latest - facts[4], facts[2 + c] * STRETCH)
        peaks, totals = [], []
        for j in range(CHUNKS):
            rows = pl.ds(j * CHUNK, CHUNK)
            raw = dot(window[rows], q, (1, 1))
            row = lax.broadcasted_iota(jnp.int32, (CHUNK, COLS), 0) + j * CHUNK
            seen = row >= earliest
            if (j + 1) * CHUNK > BACK * STRETCH:
                seen = seen & (row <= latest)
            raw = jnp.where(seen, raw * scale, FAR)
            score[c, rows] = raw
            peaks.append(jnp.max(raw, axis=0, keepdims=True))
            expd = jnp.exp2(score[c, rows] - peaks[j])
            score[c, rows] = expd
            totals.append(jnp.sum(expd, axis=0, keepdims=True))
        peak = functools.reduce(jnp.maximum, peaks)
        weights = [jnp.exp2(p - peak) for p in peaks]
        share = 1.0 / sum(w * t for w, t in zip(weights, totals))
        for j in range(CHUNKS):
            rows = pl.ds(j * CHUNK, CHUNK)
            prob = (score[c, rows] * (share * weights[j])).astype(jnp.bfloat16)
            prob_out[c, rows] = prob
            terms[c, rows] = dot(prob, g, (1, 0))
    spread(places, facts, terms, held)
    give(held, outs)


def value_kernel(places, facts, prob_in, keys_in, q_heads, g_heads, *refs):
    pieces, refs = refs[: len(ALL)], refs[len(ALL) :]
    grad_query, *outs = refs[:4]
    held, window, dprob, terms = refs[4:]
    lay(pieces[: len(PIECES)], held, pl.ds(HEAD_DIM, HEAD_DIM))
    lay(pieces[len(PIECES) :], held.at[pl.ds(SLOTS * STRETCH, 2 * TAIL * STRETCH)])
    scale = 1.0 / HEAD_DIM**0.5

    for c in range(2):
        fetch(places, c, held, window.at[c])
        q, g = q_heads[c], g_heads[c]
        delta = 0.0
        for j in range(CHUNKS):
            rows = pl.ds(j * CHUNK, CHUNK)
            dp = dot(window[c, rows], g, (1, 1))
            dprob[c, rows] = dp
            delta = delta + jnp.sum(prob_in[c, rows].astype(jnp.float32) * dp, axis=0, keepdims=True)
        dq = 0.0
        for j in range(CHUNKS):
            rows = pl.ds(j * CHUNK, CHUNK)
            prob = prob_in[c, rows].astype(jnp.float32)
            dscore = (prob * (dprob[c, rows] - delta)).astype(jnp.bfloat16)
            terms[c, rows] = dot(dscore, q, (1, 0)) * scale
            dq = dq + dot(keys_in[c, rows], dscore, (0, 0))
        dq = (jnp.transpose(dq) * scale).astype(jnp.bfloat16)
        for h in range(HEADS):
            grad_query[pl.ds(c * STRETCH, STRETCH), pl.ds(h * HEAD_DIM, HEAD_DIM)] = dq[
                h * STRETCH : (h + 1) * STRETCH
            ]
    spread(places, facts, terms, held)
    give(held, outs)


PIECE_SHAPES = tuple(shape(n * STRETCH, 2 * HEAD_DIM) for n in PIECES)
TERM_SHAPES = (shape(SLOTS * STRETCH), shape(TAIL * STRETCH), shape(TAIL * STRETCH))
HEAD_SHAPE = jax.ShapeDtypeStruct((2, COLS, HEAD_DIM), jnp.bfloat16)


def cost(matmuls):
    return pl.CostEstimate(
        flops=matmuls * 4 * WINDOW * COLS * HEAD_DIM, bytes_accessed=matmuls * 2**21, transcendentals=0
    )


def on_keys(places, facts, query, grad_out, pieces):
    return pl.pallas_call(
        key_kernel,
        out_shape=(
            jax.ShapeDtypeStruct((2, WINDOW, COLS), jnp.bfloat16),
            jax.ShapeDtypeStruct((2, WINDOW, HEAD_DIM), jnp.bfloat16),
            HEAD_SHAPE,
            HEAD_SHAPE,
        )
        + TERM_SHAPES,
        in_specs=[SMEM, SMEM] + [VMEM] * (2 + len(pieces)),
        out_specs=(VMEM,) * 7,
        scratch_shapes=[
            pltpu.VMEM(((SLOTS + BACK + 1) * STRETCH, HEAD_DIM), jnp.bfloat16),
            pltpu.VMEM((2, WINDOW, COLS), jnp.float32),
            pltpu.VMEM((2, WINDOW, HEAD_DIM), jnp.float32),
        ],
        compiler_params=pltpu.CompilerParams(vmem_limit_bytes=VMEM_LIMIT),
        cost_estimate=cost(KEY_COST),
        name="on_keys",
    )(places, facts, query, grad_out, *pieces)


def on_values(places, facts, carried, pieces):
    return pl.pallas_call(
        value_kernel,
        out_shape=(shape(2 * STRETCH, HEADS * HEAD_DIM),) + TERM_SHAPES,
        in_specs=[SMEM, SMEM] + [VMEM] * (4 + len(pieces)),
        out_specs=(VMEM,) * 4,
        scratch_shapes=[
            pltpu.VMEM(((SLOTS + BACK + 1) * STRETCH, HEAD_DIM), jnp.bfloat16),
            pltpu.VMEM((2, WINDOW, HEAD_DIM), jnp.bfloat16),
            pltpu.VMEM((2, WINDOW, COLS), jnp.float32),
            pltpu.VMEM((2, WINDOW, HEAD_DIM), jnp.float32),
        ],
        compiler_params=pltpu.CompilerParams(vmem_limit_bytes=VMEM_LIMIT),
        cost_estimate=cost(VALUE_COST),
        name="on_values",
    )(places, facts, *carried, *pieces)


def merge_kernel(places, keys, values, tail_keys, tail_values, *refs):
    outs, held = refs[:-1], refs[-1]
    for i, (block, tail) in enumerate(((keys, tail_keys), (values, tail_values))):
        columns = pl.ds(i * HEAD_DIM, HEAD_DIM)
        held[:, columns] = block[...]

        def one(j, carry, tail=tail, columns=columns):
            rows = at(places[j])
            total = held[rows, columns].astype(jnp.float32) + tail[at(j)].astype(jnp.float32)
            held[rows, columns] = total.astype(jnp.bfloat16)
            return carry

        lax.fori_loop(0, TAIL, one, 0)
    give(held, outs)


def merge(places, *arrays):
    return pl.pallas_call(
        merge_kernel,
        out_shape=PIECE_SHAPES,
        in_specs=[SMEM] + [VMEM] * len(arrays),
        out_specs=(VMEM,) * len(PIECES),
        scratch_shapes=[pltpu.VMEM((SLOTS * STRETCH, 2 * HEAD_DIM), jnp.bfloat16)],
        compiler_params=small(MERGE_KIB),
        name="merge_tail",
    )(places, *arrays)


def join(parts):
    return jnp.concatenate(parts, 0)


def wide(value):
    return value.astype(jnp.float32)


def reduce_block(pieces, unit):
    own, other = pieces[:5], pieces[5:]
    arrived = [swap(piece) for piece in other]
    sums = [wide(a) + wide(b) for a, b in zip(own, arrived)]
    mine, up, down, ahead, behind = [sums[0]] + [s.astype(jnp.bfloat16) for s in sums[1:]]
    up, down = shift(up, 0, -1), shift(down, 0, 1)
    ahead, behind = shift(ahead, -1, 0), shift(behind, 1, 0)
    half = ahead.shape[0]
    mine = mine + wide(up) + wide(down)
    mine = jnp.concatenate([mine[:half] + wide(ahead) + wide(behind), mine[half:]], 0)
    mine_b = mine.astype(jnp.bfloat16)
    home = [tuple((-dz, -dy) for dz, dy in m) for m in MEMBERS]
    first = send(mine_b[3 * unit : 6 * unit], home[0])
    second, third = send(mine_b[unit : 3 * unit], home[1]), send(mine_b[6 * unit :], home[2])
    opposite = send(first[:unit], home[0])
    there = wide(first[2 * unit :]) + wide(second[unit:]) + wide(third[unit:])
    here = mine[:unit] + wide(opposite) + wide(first[unit : 2 * unit]) + wide(second[:unit]) + wide(third[:unit])
    return here + wide(swap(there.astype(jnp.bfloat16)))


def per_device(query, key, value, grad_out, stretch_order, reach):
    unit = query.shape[0]
    nodes = lax.axis_size("node")
    onward = [(n, (n + 1) % nodes) for n in range(nodes)]
    backward = [((n + 1) % nodes, n) for n in range(nodes)]
    tables = []

    def settle(early, late):
        tables.extend(plan(stretch_order, lax.optimization_barrier((reach, early))[0]))
        late, *tables[:] = lax.optimization_barrier((late, *tables))
        return late

    pieces = gather_block(jnp.concatenate([key, value], axis=1), unit, send, join, settle)
    places, tail_places, facts = tables
    tails = [lax.ppermute(tail, "node", onward) for tail in pick(tail_places, pieces)]
    keys, values = [pieces + [tail, swap(tail)] for tail in tails]

    *carried, block_values, own_tail, other_tail = on_keys(places, facts, query, grad_out, keys)
    tail_values = (wide(own_tail) + wide(swap(other_tail))).astype(jnp.bfloat16)
    carried[0], tail_values = lax.optimization_barrier((carried[0], tail_values))
    tail_values = lax.ppermute(tail_values, "node", backward)
    grad_query, block_keys, own_tail, other_tail = on_values(places, facts, carried, values)
    tail_values, own_tail, other_tail = lax.optimization_barrier((tail_values, own_tail, other_tail))
    tail_keys = (wide(own_tail) + wide(swap(other_tail))).astype(jnp.bfloat16)
    tail_keys = lax.ppermute(tail_keys, "node", backward)
    pieces = merge(tail_places, block_keys, block_values, tail_keys, tail_values)
    sums = reduce_block(pieces, unit).astype(jnp.bfloat16)
    return grad_query, sums[:, :HEAD_DIM], sums[:, HEAD_DIM:]


def solution(mesh):
    rows = P(("node", "local"), None)
    return jax.shard_map(
        per_device,
        mesh=mesh,
        in_specs=(rows, rows, rows, rows, P(), P()),
        out_specs=(rows, rows, rows),
        check_vma=False,
    )
```

```python
import functools

import jax
import jax.numpy as jnp
import numpy as np
from jax import lax
from jax.experimental import pallas as pl
from jax.experimental.pallas import tpu as pltpu
from jax.sharding import PartitionSpec as P

HEAD_DIM = 128
HEADS = 8
STRETCH = 64
SLOTS = 128
BACK = 32
KEYS = BACK + 1
WINDOW = KEYS * STRETCH
COLS = HEADS * STRETCH
CHUNK = 11 * STRETCH
CHUNKS = WINDOW // CHUNK
TAIL = BACK // 2
NZ, NY = 8, 4
LOCAL = NZ * NY * 2
FAR = -1e30

MEMBERS = (((2, 0), (6, 0)), ((1, 2), (5, 2)), ((3, 2), (7, 2)))


def local_of(z, y, c):
    return ((z % NZ) * NY + y % NY) * 2 + c


def moves(by_core):
    out = []
    for source in range(LOCAL):
        z, y, c = source // (NY * 2), (source // 2) % NY, source % 2
        if by_core is None:
            out.append((source, local_of(z, y, 1 - c)))
        else:
            dz, dy = by_core[c]
            out.append((source, local_of(z + dz, y + dy, c)))
    return out


def send(value, by_core):
    return lax.ppermute(value, "local", moves(by_core))


def swap(value):
    return send(value, None)


def shift(value, dz, dy):
    return send(value, ((dz, dy), (dz, dy)))


def gather_block(own, other, unit, send, join, settle=lambda early, late: late):
    swap = functools.partial(send, by_core=None)
    chip = join([own, other])
    first, second, third = [send(chip, by_core=m) for m in MEMBERS]
    opposite = send(first[:unit], by_core=MEMBERS[0])
    mine = join([own, second, settle(first, opposite), first, third])
    half = 4 * unit
    up, down = [send(mine, by_core=((0, dy), (0, dy))) for dy in (1, -1)]
    ahead, behind = [send(mine[:half], by_core=((dz, 0), (dz, 0))) for dz in (1, -1)]
    pieces = [mine, up, down, ahead, behind]
    return pieces + [swap(piece) for piece in pieces]


def piece_table():
    labels = np.arange(SLOTS).reshape(LOCAL, 2).T

    def fake_send(value, by_core):
        out = np.empty_like(value)
        for source, target in moves(by_core):
            out[:, target] = value[:, source]
        return out

    pieces = gather_block(labels, fake_send(labels, None), 2, fake_send, lambda parts: np.concatenate(parts, 0))
    order = np.concatenate(pieces, 0).T
    table = np.empty((LOCAL, SLOTS), np.int32)
    for device in range(LOCAL):
        table[device, order[device]] = np.arange(SLOTS)
    return table


TABLE = piece_table()
PIECES = (16, 16, 16, 8, 8) * 2
ALL = PIECES + (TAIL, TAIL)
STARTS = tuple(int(s) for s in np.cumsum((0,) + ALL))
KEY_COST = 0
VALUE_COST = 6
VMEM_LIMIT = 36 * 2**20
PICK_KIB = 12 * 1024
MERGE_KIB = 16 * 1024

SMEM = pl.BlockSpec(memory_space=pltpu.SMEM)
VMEM = pl.BlockSpec(memory_space=pltpu.VMEM)


def at(i, size=STRETCH):
    return pl.ds(pl.multiple_of(i * size, size), size)


def shape(rows, columns=HEAD_DIM, dtype=jnp.bfloat16):
    return jax.ShapeDtypeStruct((rows, columns), dtype)


def lay(refs, held, columns=slice(None)):
    first = 0
    for ref in refs:
        held[pl.ds(first, ref.shape[0])] = ref[:, columns]
        first += ref.shape[0]


def small(kib):
    return pltpu.CompilerParams(vmem_limit_bytes=kib * 1024)


def plan_kernel(order, reach, table, places, tail_places, facts, inverse):
    node, local = lax.axis_index("node"), lax.axis_index("local")
    core = local % 2

    def turn(s, carry):
        inverse[order[node, s]] = table[local, s]
        return carry

    lax.fori_loop(0, SLOTS, turn, 0, unroll=8)
    for i in range(TAIL):
        tail_places[i] = inverse[SLOTS - BACK + core * TAIL + i]
    facts[4] = reach[node]
    for c in range(2):
        own = order[node, 2 * local + c]
        facts[c] = own
        first = jnp.where(node > 0, 0, jnp.maximum(BACK - own, 0))
        facts[2 + c] = first

        def find(k, carry, c=c, own=own):
            wanted = own - BACK + k
            tail = jnp.maximum(wanted + BACK, 0)
            half = tail // TAIL
            in_tail = SLOTS + jnp.where(half == core, 0, TAIL) + tail % TAIL
            now = inverse[jnp.maximum(wanted, 0)]
            places[c * KEYS + k] = jnp.where(wanted >= 0, now, jnp.where(node > 0, in_tail, 0))
            return carry

        lax.fori_loop(0, KEYS, find, 0, unroll=3)


def plan(stretch_order, reach):
    return pl.pallas_call(
        plan_kernel,
        out_shape=tuple(jax.ShapeDtypeStruct((n,), jnp.int32) for n in (2 * KEYS, TAIL, 5)),
        in_specs=[SMEM] * 3,
        out_specs=(SMEM,) * 3,
        scratch_shapes=[pltpu.SMEM((SLOTS,), jnp.int32)],
        compiler_params=small(256),
        name="plan",
    )(stretch_order, reach, jnp.asarray(TABLE))


def pick_kernel(places, *refs):
    pieces, keys, values, held = refs[: len(PIECES)], *refs[len(PIECES) :]
    lay(pieces, held)

    def one(i, carry):
        rows = held[at(places[i])]
        keys[at(i)], values[at(i)] = rows[:, :HEAD_DIM], rows[:, HEAD_DIM:]
        return carry

    lax.fori_loop(0, TAIL, one, 0)


def pick(places, pieces):
    return pl.pallas_call(
        pick_kernel,
        out_shape=(shape(TAIL * STRETCH),) * 2,
        in_specs=[SMEM] + [VMEM] * len(pieces),
        out_specs=(VMEM,) * 2,
        scratch_shapes=[pltpu.VMEM((SLOTS * STRETCH, 2 * HEAD_DIM), jnp.bfloat16)],
        compiler_params=small(PICK_KIB),
        name="pick_tail",
    )(places, *pieces)


def stack_heads(array, heads):
    for c in range(2):
        for h in range(HEADS):
            heads[c, pl.ds(h * STRETCH, STRETCH)] = array[
                pl.ds(c * STRETCH, STRETCH), pl.ds(h * HEAD_DIM, HEAD_DIM)
            ]


def fetch(places, c, held, window):
    def one(k, carry):
        window[at(k)] = held[at(places[c * KEYS + k])]
        return carry

    lax.fori_loop(0, KEYS, one, 0, unroll=11)


def spread(places, facts, terms, held):
    def clear(i, carry):
        held[at(i, 256)] = jnp.zeros((256, HEAD_DIM), jnp.bfloat16)
        return carry

    lax.fori_loop(0, held.shape[0] // 256, clear, 0, unroll=8)

    dump = SLOTS + BACK

    def first(k, carry):
        place = jnp.where(k >= facts[2], places[k], dump)
        held[at(place)] = terms[0, at(k)].astype(jnp.bfloat16)
        return carry

    lax.fori_loop(0, KEYS, first, 0, unroll=11)

    def second(k, carry):
        place = jnp.where(k >= facts[3], places[KEYS + k], dump)
        twin = k + facts[1] - facts[0]
        both = (twin >= facts[2]) & (twin < KEYS)
        twin = jnp.clip(twin, 0, KEYS - 1)
        term = terms[1, at(k)] + jnp.where(both, terms[0, at(twin)], 0.0)
        held[at(place)] = term.astype(jnp.bfloat16)
        return carry

    lax.fori_loop(0, KEYS, second, 0, unroll=11)


def give(held, outs, first=0):
    for out in outs:
        out[...] = held[pl.ds(first, out.shape[0])]
        first += out.shape[0]


def dot(a, b, over):
    return lax.dot_general(a, b, ((over[:1], over[1:]), ((), ())), preferred_element_type=jnp.float32)


def key_kernel(places, facts, query, grad_out, *refs):
    pieces, refs = refs[: len(ALL)], refs[len(ALL) :]
    prob_out, keys_out, q_heads, g_heads, held, *outs = refs[:7]
    score, terms = refs[7:]
    lay(pieces, held, pl.ds(0, HEAD_DIM))
    scale = 1.4426950408889634 / HEAD_DIM**0.5
    stack_heads(query, q_heads)
    stack_heads(grad_out, g_heads)
    token = lax.broadcasted_iota(jnp.int32, (1, COLS), 1) % STRETCH
    latest = BACK * STRETCH + token

    def stretch(c, carry):
        window = keys_out.at[c]
        fetch(places, c, held, window)
        q, g = q_heads[c], g_heads[c]
        earliest = jnp.maximum(latest - facts[4], facts[2 + c] * STRETCH)
        peaks, totals = [], []
        for j in range(CHUNKS):
            rows = pl.ds(j * CHUNK, CHUNK)
            raw = dot(window[rows], q, (1, 1))
            row = lax.broadcasted_iota(jnp.int32, (CHUNK, COLS), 0) + j * CHUNK
            seen = row >= earliest
            if (j + 1) * CHUNK > BACK * STRETCH:
                seen = seen & (row <= latest)
            raw = jnp.where(seen, raw * scale, FAR)
            score[c, rows] = raw
            peaks.append(jnp.max(raw, axis=0, keepdims=True))
            expd = jnp.exp2(score[c, rows] - peaks[j])
            score[c, rows] = expd
            totals.append(jnp.sum(expd, axis=0, keepdims=True))
        peak = functools.reduce(jnp.maximum, peaks)
        weights = [jnp.exp2(p - peak) for p in peaks]
        share = 1.0 / sum(w * t for w, t in zip(weights, totals))
        for j in range(CHUNKS):
            rows = pl.ds(j * CHUNK, CHUNK)
            prob = (score[c, rows] * (share * weights[j])).astype(jnp.bfloat16)
            prob_out[c, rows] = prob
            terms[c, rows] = dot(prob, g, (1, 0))
        return carry

    lax.fori_loop(0, 2, stretch, 0)
    spread(places, facts, terms, held)
    give(held, outs, SLOTS * STRETCH)


def value_kernel(places, facts, prob_in, keys_in, q_heads, g_heads, *refs):
    pieces, refs = refs[: len(ALL)], refs[len(ALL) :]
    grad_query, held, *outs = refs[:4]
    window, dprob, terms = refs[4:]
    lay(pieces[: len(PIECES)], held, pl.ds(HEAD_DIM, HEAD_DIM))
    lay(pieces[len(PIECES) :], held.at[pl.ds(SLOTS * STRETCH, 2 * TAIL * STRETCH)])
    scale = 1.0 / HEAD_DIM**0.5

    def stretch(c, carry):
        fetch(places, c, held, window.at[c])
        q, g = q_heads[c], g_heads[c]
        delta = 0.0
        for j in range(CHUNKS):
            rows = pl.ds(j * CHUNK, CHUNK)
            dp = dot(window[c, rows], g, (1, 1))
            dprob[c, rows] = dp
            delta = delta + jnp.sum(prob_in[c, rows].astype(jnp.float32) * dp, axis=0, keepdims=True)
        dq = 0.0
        for j in range(CHUNKS):
            rows = pl.ds(j * CHUNK, CHUNK)
            prob = prob_in[c, rows].astype(jnp.float32)
            dscore = (prob * (dprob[c, rows] - delta)).astype(jnp.bfloat16)
            terms[c, rows] = dot(dscore, q, (1, 0)) * scale
            dq = dq + dot(keys_in[c, rows], dscore, (0, 0))
        dq = (jnp.transpose(dq) * scale).astype(jnp.bfloat16)
        for h in range(HEADS):
            grad_query[at(c), pl.ds(h * HEAD_DIM, HEAD_DIM)] = dq[
                h * STRETCH : (h + 1) * STRETCH
            ]
        return carry

    lax.fori_loop(0, 2, stretch, 0)
    spread(places, facts, terms, held)
    give(held, outs, SLOTS * STRETCH)


PIECE_SHAPES = tuple(shape(n * STRETCH, 2 * HEAD_DIM) for n in PIECES)
TERM_SHAPES = (shape((SLOTS + BACK + 1) * STRETCH), shape(TAIL * STRETCH), shape(TAIL * STRETCH))
HEAD_SHAPE = jax.ShapeDtypeStruct((2, COLS, HEAD_DIM), jnp.bfloat16)


def cost(matmuls):
    return pl.CostEstimate(
        flops=matmuls * 4 * WINDOW * COLS * HEAD_DIM, bytes_accessed=matmuls * 2**21, transcendentals=0
    )


def on_keys(places, facts, query, grad_out, pieces):
    return pl.pallas_call(
        key_kernel,
        out_shape=(
            jax.ShapeDtypeStruct((2, WINDOW, COLS), jnp.bfloat16),
            jax.ShapeDtypeStruct((2, WINDOW, HEAD_DIM), jnp.bfloat16),
            HEAD_SHAPE,
            HEAD_SHAPE,
        )
        + TERM_SHAPES,
        in_specs=[SMEM, SMEM] + [VMEM] * (2 + len(pieces)),
        out_specs=(VMEM,) * 7,
        scratch_shapes=[
            pltpu.VMEM((2, WINDOW, COLS), jnp.float32),
            pltpu.VMEM((2, WINDOW, HEAD_DIM), jnp.float32),
        ],
        compiler_params=pltpu.CompilerParams(vmem_limit_bytes=VMEM_LIMIT),
        cost_estimate=cost(KEY_COST),
        name="on_keys",
    )(places, facts, query, grad_out, *pieces)


def on_values(places, facts, carried, pieces):
    return pl.pallas_call(
        value_kernel,
        out_shape=(shape(2 * STRETCH, HEADS * HEAD_DIM),) + TERM_SHAPES,
        in_specs=[SMEM, SMEM] + [VMEM] * (4 + len(pieces)),
        out_specs=(VMEM,) * 4,
        scratch_shapes=[
            pltpu.VMEM((2, WINDOW, HEAD_DIM), jnp.bfloat16),
            pltpu.VMEM((2, WINDOW, COLS), jnp.float32),
            pltpu.VMEM((2, WINDOW, HEAD_DIM), jnp.float32),
        ],
        compiler_params=pltpu.CompilerParams(vmem_limit_bytes=VMEM_LIMIT),
        cost_estimate=cost(VALUE_COST),
        name="on_values",
    )(places, facts, *carried, *pieces)


def merge_kernel(places, keys, values, tail_keys, tail_values, *refs):
    outs, held = refs[:-1], refs[-1]
    for i, (block, tail) in enumerate(((keys, tail_keys), (values, tail_values))):
        columns = pl.ds(i * HEAD_DIM, HEAD_DIM)
        held[:, columns] = block[: SLOTS * STRETCH]

        def one(j, carry, tail=tail, columns=columns):
            rows = at(places[j])
            total = held[rows, columns].astype(jnp.float32) + tail[at(j)].astype(jnp.float32)
            held[rows, columns] = total.astype(jnp.bfloat16)
            return carry

        lax.fori_loop(0, TAIL, one, 0)
    give(held, outs)


def merge(places, *arrays):
    return pl.pallas_call(
        merge_kernel,
        out_shape=PIECE_SHAPES,
        in_specs=[SMEM] + [VMEM] * len(arrays),
        out_specs=(VMEM,) * len(PIECES),
        scratch_shapes=[pltpu.VMEM((SLOTS * STRETCH, 2 * HEAD_DIM), jnp.bfloat16)],
        compiler_params=small(MERGE_KIB),
        name="merge_tail",
    )(places, *arrays)


def join(parts):
    return jnp.concatenate(parts, 0)


def wide(value):
    return value.astype(jnp.float32)


def reduce_block(pieces, unit):
    own, other = pieces[:5], pieces[5:]
    arrived = [swap(piece) for piece in other]
    sums = [wide(a) + wide(b) for a, b in zip(own, arrived)]
    mine, up, down, ahead, behind = [sums[0]] + [s.astype(jnp.bfloat16) for s in sums[1:]]
    up, down = shift(up, 0, -1), shift(down, 0, 1)
    ahead, behind = shift(ahead, -1, 0), shift(behind, 1, 0)
    half = ahead.shape[0]
    mine = mine + wide(up) + wide(down)
    mine = jnp.concatenate([mine[:half] + wide(ahead) + wide(behind), mine[half:]], 0)
    mine_b = mine.astype(jnp.bfloat16)
    home = [tuple((-dz, -dy) for dz, dy in m) for m in MEMBERS]
    first = send(mine_b[3 * unit : 6 * unit], home[0])
    second, third = send(mine_b[unit : 3 * unit], home[1]), send(mine_b[6 * unit :], home[2])
    opposite = send(first[:unit], home[0])
    there = wide(first[2 * unit :]) + wide(second[unit:]) + wide(third[unit:])
    here = mine[:unit] + wide(opposite) + wide(first[unit : 2 * unit]) + wide(second[:unit]) + wide(third[:unit])
    return here + wide(swap(there.astype(jnp.bfloat16)))


def per_device(query, key, value, grad_out, stretch_order, reach):
    unit = query.shape[0]
    nodes = lax.axis_size("node")
    onward = [(n, (n + 1) % nodes) for n in range(nodes)]
    backward = [((n + 1) % nodes, n) for n in range(nodes)]
    tables = []

    def settle(early, late):
        tables.extend(plan(stretch_order, lax.optimization_barrier((reach, early))[0]))
        late, *tables[:] = lax.optimization_barrier((late, *tables))
        return late

    own, other = [jnp.concatenate(rows, axis=1) for rows in ((key, value), (swap(key), swap(value)))]
    pieces = gather_block(own, other, unit, send, join, settle)
    places, tail_places, facts = tables
    tails = [lax.ppermute(tail, "node", onward) for tail in pick(tail_places, pieces)]
    keys, values = [pieces + [tail, swap(tail)] for tail in tails]

    *carried, block_values, own_tail, other_tail = on_keys(places, facts, query, grad_out, keys)
    tail_values = (wide(own_tail) + wide(swap(other_tail))).astype(jnp.bfloat16)
    carried[0], tail_values = lax.optimization_barrier((carried[0], tail_values))
    tail_values = lax.ppermute(tail_values, "node", backward)
    grad_query, block_keys, own_tail, other_tail = on_values(places, facts, carried, values)
    tail_values, own_tail, other_tail = lax.optimization_barrier((tail_values, own_tail, other_tail))
    tail_keys = (wide(own_tail) + wide(swap(other_tail))).astype(jnp.bfloat16)
    tail_keys = lax.ppermute(tail_keys, "node", backward)
    pieces = merge(tail_places, block_keys, block_values, tail_keys, tail_values)
    sums = reduce_block(pieces, unit).astype(jnp.bfloat16)
    return grad_query, sums[:, :HEAD_DIM], sums[:, HEAD_DIM:]


def solution(mesh):
    rows = P(("node", "local"), None)
    return jax.shard_map(
        per_device,
        mesh=mesh,
        in_specs=(rows, rows, rows, rows, P(), P()),
        out_specs=(rows, rows, rows),
        check_vma=False,
    )
```

```python
import functools

import jax
import jax.numpy as jnp
import numpy as np
from jax import lax
from jax.experimental import pallas as pl
from jax.experimental.pallas import tpu as pltpu
from jax.sharding import PartitionSpec as P

HEAD_DIM = 128
HEADS = 8
STRETCH = 64
SLOTS = 128
BACK = 32
KEYS = BACK + 1
WINDOW = KEYS * STRETCH
COLS = HEADS * STRETCH
CHUNK = 11 * STRETCH
CHUNKS = WINDOW // CHUNK
TAIL = BACK // 2
NZ, NY = 8, 4
LOCAL = NZ * NY * 2
FAR = -1e30

MEMBERS = (((2, 0), (6, 0)), ((1, 2), (5, 2)), ((3, 2), (7, 2)))


def local_of(z, y, c):
    return ((z % NZ) * NY + y % NY) * 2 + c


def moves(by_core):
    out = []
    for source in range(LOCAL):
        z, y, c = source // (NY * 2), (source // 2) % NY, source % 2
        if by_core is None:
            out.append((source, local_of(z, y, 1 - c)))
        else:
            dz, dy = by_core[c]
            out.append((source, local_of(z + dz, y + dy, c)))
    return out


def send(value, by_core):
    return lax.ppermute(value, "local", moves(by_core))


def swap(value):
    return send(value, None)


def shift(value, dz, dy):
    return send(value, ((dz, dy), (dz, dy)))


def gather_block(own, other, unit, send, join, settle=lambda early, late: late):
    swap = functools.partial(send, by_core=None)
    chip = join([own, other])
    first, second, third = [send(chip, by_core=m) for m in MEMBERS]
    opposite = send(first[:unit], by_core=MEMBERS[0])
    mine = join([own, second, settle(first, opposite), first, third])
    half = 4 * unit
    up, down = [send(mine, by_core=((0, dy), (0, dy))) for dy in (1, -1)]
    ahead, behind = [send(mine[:half], by_core=((dz, 0), (dz, 0))) for dz in (1, -1)]
    pieces = [mine, up, down, ahead, behind]
    return pieces + [swap(piece) for piece in pieces]


def piece_table():
    labels = np.arange(SLOTS).reshape(LOCAL, 2).T

    def fake_send(value, by_core):
        out = np.empty_like(value)
        for source, target in moves(by_core):
            out[:, target] = value[:, source]
        return out

    pieces = gather_block(labels, fake_send(labels, None), 2, fake_send, lambda parts: np.concatenate(parts, 0))
    order = np.concatenate(pieces, 0).T
    table = np.empty((LOCAL, SLOTS), np.int32)
    for device in range(LOCAL):
        table[device, order[device]] = np.arange(SLOTS)
    return table


TABLE = piece_table()
PIECES = (16, 16, 16, 8, 8) * 2
ALL = PIECES + (TAIL, TAIL)
STARTS = tuple(int(s) for s in np.cumsum((0,) + ALL))
KEY_COST = 0
VALUE_COST = 6
VMEM_LIMIT = 36 * 2**20
PICK_KIB = 12 * 1024
MERGE_KIB = 16 * 1024

SMEM = pl.BlockSpec(memory_space=pltpu.SMEM)
VMEM = pl.BlockSpec(memory_space=pltpu.VMEM)


def at(i, size=STRETCH):
    return pl.ds(pl.multiple_of(i * size, size), size)


def shape(rows, columns=HEAD_DIM, dtype=jnp.bfloat16):
    return jax.ShapeDtypeStruct((rows, columns), dtype)


def lay(refs, held, columns=slice(None)):
    first = 0
    for ref in refs:
        held[pl.ds(first, ref.shape[0])] = ref[:, columns]
        first += ref.shape[0]


def small(kib):
    return pltpu.CompilerParams(vmem_limit_bytes=kib * 1024)


def plan_kernel(order, reach, table, places, tail_places, facts, inverse):
    node, local = lax.axis_index("node"), lax.axis_index("local")
    core = local % 2

    def turn(s, carry):
        inverse[order[node, s]] = table[local, s]
        return carry

    lax.fori_loop(0, SLOTS, turn, 0, unroll=8)
    for i in range(TAIL):
        tail_places[i] = inverse[SLOTS - BACK + core * TAIL + i]
    facts[4] = reach[node]
    for c in range(2):
        own = order[node, 2 * local + c]
        facts[c] = own
        first = jnp.where(node > 0, 0, jnp.maximum(BACK - own, 0))
        facts[2 + c] = first

        def find(k, carry, c=c, own=own):
            wanted = own - BACK + k
            tail = jnp.maximum(wanted + BACK, 0)
            half = tail // TAIL
            in_tail = SLOTS + jnp.where(half == core, 0, TAIL) + tail % TAIL
            now = inverse[jnp.maximum(wanted, 0)]
            places[c * KEYS + k] = jnp.where(wanted >= 0, now, jnp.where(node > 0, in_tail, 0))
            return carry

        lax.fori_loop(0, KEYS, find, 0, unroll=3)


def plan(stretch_order, reach):
    return pl.pallas_call(
        plan_kernel,
        out_shape=tuple(jax.ShapeDtypeStruct((n,), jnp.int32) for n in (2 * KEYS, TAIL, 5)),
        in_specs=[SMEM] * 3,
        out_specs=(SMEM,) * 3,
        scratch_shapes=[pltpu.SMEM((SLOTS,), jnp.int32)],
        compiler_params=small(256),
        name="plan",
    )(stretch_order, reach, jnp.asarray(TABLE))


def pick_kernel(part, places, *refs):
    pieces, (out, held) = refs[: len(PIECES)], refs[len(PIECES) :]
    lay(pieces, held, pl.ds(part * HEAD_DIM, HEAD_DIM))

    def one(i, carry):
        out[at(i)] = held[at(places[i])]
        return carry

    lax.fori_loop(0, TAIL, one, 0, unroll=4)


def pick(part, places, pieces):
    return pl.pallas_call(
        functools.partial(pick_kernel, part),
        out_shape=shape(TAIL * STRETCH),
        in_specs=[SMEM] + [VMEM] * len(pieces),
        out_specs=VMEM,
        scratch_shapes=[pltpu.VMEM((SLOTS * STRETCH, HEAD_DIM), jnp.bfloat16)],
        compiler_params=small(PICK_KIB),
        name="pick_tail",
    )(places, *pieces)


def stack_heads(array, heads):
    for c in range(2):
        for h in range(HEADS):
            heads[c, pl.ds(h * STRETCH, STRETCH)] = array[
                pl.ds(c * STRETCH, STRETCH), pl.ds(h * HEAD_DIM, HEAD_DIM)
            ]


def fetch(places, c, held, window):
    def one(k, carry):
        window[at(k)] = held[at(places[c * KEYS + k])]
        return carry

    lax.fori_loop(0, KEYS, one, 0, unroll=11)


def spread(places, facts, terms, held):
    def clear(i, carry):
        held[at(i, 256)] = jnp.zeros((256, HEAD_DIM), jnp.bfloat16)
        return carry

    lax.fori_loop(0, held.shape[0] // 256, clear, 0, unroll=8)

    dump = SLOTS + BACK

    def first(k, carry):
        place = jnp.where(k >= facts[2], places[k], dump)
        held[at(place)] = terms[0, at(k)].astype(jnp.bfloat16)
        return carry

    lax.fori_loop(0, KEYS, first, 0, unroll=11)

    def second(k, carry):
        place = jnp.where(k >= facts[3], places[KEYS + k], dump)
        twin = k + facts[1] - facts[0]
        both = (twin >= facts[2]) & (twin < KEYS)
        twin = jnp.clip(twin, 0, KEYS - 1)
        term = terms[1, at(k)] + jnp.where(both, terms[0, at(twin)], 0.0)
        held[at(place)] = term.astype(jnp.bfloat16)
        return carry

    lax.fori_loop(0, KEYS, second, 0, unroll=11)


def give(held, outs, first=0):
    for out in outs:
        out[...] = held[pl.ds(first, out.shape[0])]
        first += out.shape[0]


def dot(a, b, over):
    return lax.dot_general(a, b, ((over[:1], over[1:]), ((), ())), preferred_element_type=jnp.float32)


def key_kernel(places, facts, query, grad_out, *refs):
    pieces, refs = refs[: len(ALL)], refs[len(ALL) :]
    prob_out, keys_out, q_heads, g_heads, held, *outs = refs[:7]
    score, terms = refs[7:]
    lay(pieces, held, pl.ds(0, HEAD_DIM))
    scale = 1.4426950408889634 / HEAD_DIM**0.5
    stack_heads(query, q_heads)
    stack_heads(grad_out, g_heads)
    token = lax.broadcasted_iota(jnp.int32, (1, COLS), 1) % STRETCH
    latest = BACK * STRETCH + token

    def stretch(c, carry):
        window = keys_out.at[c]
        fetch(places, c, held, window)
        q, g = q_heads[c], g_heads[c]
        earliest = jnp.maximum(latest - facts[4], facts[2 + c] * STRETCH)
        peaks, totals = [], []
        for j in range(CHUNKS):
            rows = pl.ds(j * CHUNK, CHUNK)
            raw = dot(window[rows], q, (1, 1))
            row = lax.broadcasted_iota(jnp.int32, (CHUNK, COLS), 0) + j * CHUNK
            seen = row >= earliest
            if (j + 1) * CHUNK > BACK * STRETCH:
                seen = seen & (row <= latest)
            raw = jnp.where(seen, raw * scale, FAR)
            score[c, rows] = raw
            peaks.append(jnp.max(raw, axis=0, keepdims=True))
            expd = jnp.exp2(score[c, rows] - peaks[j])
            score[c, rows] = expd
            totals.append(jnp.sum(expd, axis=0, keepdims=True))
        peak = functools.reduce(jnp.maximum, peaks)
        weights = [jnp.exp2(p - peak) for p in peaks]
        share = 1.0 / sum(w * t for w, t in zip(weights, totals))
        for j in range(CHUNKS):
            rows = pl.ds(j * CHUNK, CHUNK)
            prob = (score[c, rows] * (share * weights[j])).astype(jnp.bfloat16)
            prob_out[c, rows] = prob
            terms[c, rows] = dot(prob, g, (1, 0))
        return carry

    lax.fori_loop(0, 2, stretch, 0)
    spread(places, facts, terms, held)
    give(held, outs, SLOTS * STRETCH)


def value_kernel(places, facts, prob_in, keys_in, q_heads, g_heads, *refs):
    pieces, refs = refs[: len(ALL)], refs[len(ALL) :]
    grad_query, held, *outs = refs[:4]
    window, dprob, terms = refs[4:]
    lay(pieces[: len(PIECES)], held, pl.ds(HEAD_DIM, HEAD_DIM))
    lay(pieces[len(PIECES) :], held.at[pl.ds(SLOTS * STRETCH, 2 * TAIL * STRETCH)])
    scale = 1.0 / HEAD_DIM**0.5

    def stretch(c, carry):
        fetch(places, c, held, window.at[c])
        q, g = q_heads[c], g_heads[c]
        delta = 0.0
        for j in range(CHUNKS):
            rows = pl.ds(j * CHUNK, CHUNK)
            dp = dot(window[c, rows], g, (1, 1))
            dprob[c, rows] = dp
            delta = delta + jnp.sum(prob_in[c, rows].astype(jnp.float32) * dp, axis=0, keepdims=True)
        dq = 0.0
        for j in range(CHUNKS):
            rows = pl.ds(j * CHUNK, CHUNK)
            dscore = prob_in[c, rows] * (dprob[c, rows] - delta).astype(jnp.bfloat16)
            terms[c, rows] = dot(dscore, q, (1, 0)) * scale
            dq = dq + dot(keys_in[c, rows], dscore, (0, 0))
        dq = (jnp.transpose(dq) * scale).astype(jnp.bfloat16)
        for h in range(HEADS):
            grad_query[at(c), pl.ds(h * HEAD_DIM, HEAD_DIM)] = dq[
                h * STRETCH : (h + 1) * STRETCH
            ]
        return carry

    lax.fori_loop(0, 2, stretch, 0)
    spread(places, facts, terms, held)
    give(held, outs, SLOTS * STRETCH)


PIECE_SHAPES = tuple(shape(n * STRETCH, 2 * HEAD_DIM) for n in PIECES)
TERM_SHAPES = (shape((SLOTS + BACK + 1) * STRETCH), shape(TAIL * STRETCH), shape(TAIL * STRETCH))
HEAD_SHAPE = jax.ShapeDtypeStruct((2, COLS, HEAD_DIM), jnp.bfloat16)


def cost(matmuls):
    return pl.CostEstimate(
        flops=matmuls * 4 * WINDOW * COLS * HEAD_DIM, bytes_accessed=matmuls * 2**21, transcendentals=0
    )


def on_keys(places, facts, query, grad_out, pieces):
    return pl.pallas_call(
        key_kernel,
        out_shape=(
            jax.ShapeDtypeStruct((2, WINDOW, COLS), jnp.bfloat16),
            jax.ShapeDtypeStruct((2, WINDOW, HEAD_DIM), jnp.bfloat16),
            HEAD_SHAPE,
            HEAD_SHAPE,
        )
        + TERM_SHAPES,
        in_specs=[SMEM, SMEM] + [VMEM] * (2 + len(pieces)),
        out_specs=(VMEM,) * 7,
        scratch_shapes=[
            pltpu.VMEM((2, WINDOW, COLS), jnp.float32),
            pltpu.VMEM((2, WINDOW, HEAD_DIM), jnp.float32),
        ],
        compiler_params=pltpu.CompilerParams(vmem_limit_bytes=VMEM_LIMIT),
        cost_estimate=cost(KEY_COST),
        name="on_keys",
    )(places, facts, query, grad_out, *pieces)


def on_values(places, facts, carried, pieces):
    return pl.pallas_call(
        value_kernel,
        out_shape=(shape(2 * STRETCH, HEADS * HEAD_DIM),) + TERM_SHAPES,
        in_specs=[SMEM, SMEM] + [VMEM] * (4 + len(pieces)),
        out_specs=(VMEM,) * 4,
        scratch_shapes=[
            pltpu.VMEM((2, WINDOW, HEAD_DIM), jnp.bfloat16),
            pltpu.VMEM((2, WINDOW, COLS), jnp.float32),
            pltpu.VMEM((2, WINDOW, HEAD_DIM), jnp.float32),
        ],
        compiler_params=pltpu.CompilerParams(vmem_limit_bytes=VMEM_LIMIT),
        cost_estimate=cost(VALUE_COST),
        name="on_values",
    )(places, facts, *carried, *pieces)


def merge_kernel(places, keys, values, tail_keys, tail_values, *refs):
    outs, held = refs[:-1], refs[-1]
    for i, (block, tail) in enumerate(((keys, tail_keys), (values, tail_values))):
        columns = pl.ds(i * HEAD_DIM, HEAD_DIM)
        held[:, columns] = block[: SLOTS * STRETCH]

        def one(j, carry, tail=tail, columns=columns):
            rows = at(places[j])
            total = held[rows, columns].astype(jnp.float32) + tail[at(j)].astype(jnp.float32)
            held[rows, columns] = total.astype(jnp.bfloat16)
            return carry

        lax.fori_loop(0, TAIL, one, 0)
    give(held, outs)


def merge(places, *arrays):
    return pl.pallas_call(
        merge_kernel,
        out_shape=PIECE_SHAPES,
        in_specs=[SMEM] + [VMEM] * len(arrays),
        out_specs=(VMEM,) * len(PIECES),
        scratch_shapes=[pltpu.VMEM((SLOTS * STRETCH, 2 * HEAD_DIM), jnp.bfloat16)],
        compiler_params=small(MERGE_KIB),
        name="merge_tail",
    )(places, *arrays)


def join(parts):
    return jnp.concatenate(parts, 0)


def wide(value):
    return value.astype(jnp.float32)


def reduce_block(pieces, unit):
    own, other = pieces[:5], pieces[5:]
    arrived = [swap(piece) for piece in other]
    sums = [wide(a) + wide(b) for a, b in zip(own, arrived)]
    mine, up, down, ahead, behind = [sums[0]] + [s.astype(jnp.bfloat16) for s in sums[1:]]
    up, down = shift(up, 0, -1), shift(down, 0, 1)
    ahead, behind = shift(ahead, -1, 0), shift(behind, 1, 0)
    half = ahead.shape[0]
    mine = mine + wide(up) + wide(down)
    mine = jnp.concatenate([mine[:half] + wide(ahead) + wide(behind), mine[half:]], 0)
    mine_b = mine.astype(jnp.bfloat16)
    home = [tuple((-dz, -dy) for dz, dy in m) for m in MEMBERS]
    first = send(mine_b[3 * unit : 6 * unit], home[0])
    second, third = send(mine_b[unit : 3 * unit], home[1]), send(mine_b[6 * unit :], home[2])
    opposite = send(first[:unit], home[0])
    there = wide(first[2 * unit :]) + wide(second[unit:]) + wide(third[unit:])
    here = mine[:unit] + wide(opposite) + wide(first[unit : 2 * unit]) + wide(second[:unit]) + wide(third[:unit])
    return here + wide(swap(there.astype(jnp.bfloat16)))


def per_device(query, key, value, grad_out, stretch_order, reach):
    unit = query.shape[0]
    nodes = lax.axis_size("node")
    onward = [(n, (n + 1) % nodes) for n in range(nodes)]
    backward = [((n + 1) % nodes, n) for n in range(nodes)]
    tables = []

    def settle(early, late):
        tables.extend(plan(stretch_order, lax.optimization_barrier((reach, early))[0]))
        late, *tables[:] = lax.optimization_barrier((late, *tables))
        return late

    own, other = [jnp.concatenate(rows, axis=1) for rows in ((key, value), (swap(key), swap(value)))]
    pieces = gather_block(own, other, unit, send, join, settle)
    places, tail_places, facts = tables
    tails = [lax.ppermute(pick(part, tail_places, pieces), "node", onward) for part in (0, 1)]
    keys, values = [pieces + [tail, swap(tail)] for tail in tails]

    *carried, block_values, own_tail, other_tail = on_keys(places, facts, query, grad_out, keys)
    tail_values = (wide(own_tail) + wide(swap(other_tail))).astype(jnp.bfloat16)
    carried[0], tail_values = lax.optimization_barrier((carried[0], tail_values))
    tail_values = lax.ppermute(tail_values, "node", backward)
    grad_query, block_keys, own_tail, other_tail = on_values(places, facts, carried, values)
    tail_values, own_tail, other_tail = lax.optimization_barrier((tail_values, own_tail, other_tail))
    tail_keys = (wide(own_tail) + wide(swap(other_tail))).astype(jnp.bfloat16)
    tail_keys = lax.ppermute(tail_keys, "node", backward)
    pieces = merge(tail_places, block_keys, block_values, tail_keys, tail_values)
    sums = reduce_block(pieces, unit).astype(jnp.bfloat16)
    return grad_query, sums[:, :HEAD_DIM], sums[:, HEAD_DIM:]


def solution(mesh):
    rows = P(("node", "local"), None)
    return jax.shard_map(
        per_device,
        mesh=mesh,
        in_specs=(rows, rows, rows, rows, P(), P()),
        out_specs=(rows, rows, rows),
        check_vma=False,
    )
```
